128 devices in a mesh: sec: 8 (over z_lo, x), tile: 16 (over z_hi, y, core).
Axes of the slice: x: 4, y: 4, z: 4 (z_hi: 2, z_lo: 2; z = z_hi * 2 + z_lo), core: 2. Of those that a mesh axis runs over, the one named last changes fastest.
Arguments:
- sections: bfloat16 [8, 2048, 2048], P('sec', None, 'tile'), may hold values from -6 to 6
- tile_shift: int32 [8, 16, 4, 2], P('sec', 'tile'), may hold values from -4 to 4
- w_first: bfloat16 [2, 2, 1, 32], replicated, may hold values from -4 to 4
- w_second: bfloat16 [2, 2, 32, 64], replicated, may hold values from -0.75 to 0.75
- w_third: bfloat16 [2, 2, 64, 64], replicated, may hold values from -0.5 to 0.5
- w_fourth: bfloat16 [64, 64], replicated, may hold values from -1 to 1
- w_fifth: bfloat16 [64, 32], replicated, may hold values from -0.75 to 0.75
Outputs:
- correlation: bfloat16 [8, 256, 289, 256], P('sec', 'tile')
The draws below stay inside these ranges and needn't reach their ends.
All inputs are finite; a program needn't handle non-finite values.
Results may differ from the reference program's by a relative error of at most 0.0058.
Values may be sent and summed in bfloat16 or wider, within the bound.
A program may use at most 192 MiB of HBM per device.

```python
import math
import jax
import jax.numpy as jnp
from jax import lax

S = 2048
C1 = 32
C2 = 64
C3 = 64
CF = 32
REACH = 8
BOUND = 4
TILE = 16
TILE_W = 64
NSEC = 8
TY = 16
TX = 4


def place_ends(array, rng, smallest, largest):
    extent = array.shape
    index_at = [jax.random.randint(jax.random.fold_in(rng, axis), (), 0, extent[axis]) for axis in range(len(extent))]
    array = array.at[tuple(index_at)].set(smallest)
    longest = extent.index(max(extent))
    index_at[longest] = (index_at[longest] + 1) % extent[longest]
    return array.at[tuple(index_at)].set(largest)


def level_of(stream_key, dims, shards, least, high):
    loudness = 1.0
    for axis_at, blocks in shards:
        steps = jax.random.uniform(jax.random.fold_in(jax.random.fold_in(stream_key, 6), axis_at), (blocks,), jnp.float32, least / len(shards), high / len(shards))
        loudness = loudness * jnp.repeat(jnp.exp(steps), dims[axis_at] // blocks).reshape((-1,) + (1,) * (len(dims) - 1 - axis_at))
    return loudness


def bell_draw(own_key, shape, deviation, reach, shards=(), kind=jnp.bfloat16):
    entries = deviation * jax.random.normal(own_key, shape, jnp.float32)
    if shards:
        entries = entries * level_of(own_key, shape, shards, -0.22, 0.18)
    return jnp.clip(entries, -reach, reach).astype(kind)


def setup_inputs(seed: int = 0) -> dict:
    arg_keys = jax.random.split(jax.random.key(seed), 8)
    sections = bell_draw(arg_keys[0], (NSEC, S, S), 1.0, 6.0, ((0, 8), (2, 16)))
    tile_shift = place_ends(jax.random.randint(arg_keys[1], (NSEC, TY, TX, 2), -BOUND, BOUND + 1), jax.random.fold_in(arg_keys[1], 1), -BOUND, BOUND).astype(jnp.int32)
    w_first = bell_draw(arg_keys[2], (2, 2, 1, C1), 2 ** -0.5, 4.0)
    w_second = bell_draw(arg_keys[3], (2, 2, C1, C2), (2 * C1) ** -0.5, 0.75)
    w_third = bell_draw(arg_keys[4], (2, 2, C2, C3), (2 * C2) ** -0.5, 0.5)
    w_fourth = bell_draw(arg_keys[5], (C3, C3), (C3 // 2) ** -0.5, 1.0)
    w_fifth = bell_draw(arg_keys[6], (C3, CF), C3 ** -0.5, 0.75)
    return {"sections": sections, "tile_shift": tile_shift, "w_first": w_first, "w_second": w_second, "w_third": w_third, "w_fourth": w_fourth, "w_fifth": w_fifth}


def patch_layer(field, weight):
    total = None
    for row_phase in range(2):
        for col_phase in range(2):
            part = field[row_phase::2, :, col_phase::2].astype(jnp.float32)
            term = jnp.einsum('ric,io->roc', part, weight[row_phase, col_phase].astype(jnp.float32))
            total = term if total is None else total + term
    return jnp.maximum(total, 0.0).astype(jnp.bfloat16)

def point_layer(field, weight, relu):
    mixed = jnp.einsum('riw,io->row', field.astype(jnp.float32), weight.astype(jnp.float32))
    if relu:
        mixed = jnp.maximum(mixed, 0.0)
    return mixed.astype(jnp.bfloat16)

def encode(pixels, w_first, w_second, w_third, w_fourth, w_fifth):
    field = pixels[:, None, :]
    field = patch_layer(field, w_first)
    field = patch_layer(field, w_second)
    field = patch_layer(field, w_third)
    field = point_layer(field, w_fourth, True)
    return point_layer(field, w_fifth, False)

def correlate(current, source, shifts):
    rows, chans, cols = current.shape
    span = 2 * REACH + 1
    halo = REACH + BOUND
    padded = jnp.pad(source, ((0, 0), (0, 0), (halo, halo)))
    zero = jnp.zeros((), jnp.int32)

    def one_tile(row_tile, col_tile):
        shift_y = shifts[row_tile, col_tile, 0]
        shift_x = shifts[row_tile, col_tile, 1]
        here = lax.dynamic_slice(current, (row_tile * TILE, zero, col_tile * TILE_W), (TILE, chans, TILE_W)).astype(jnp.float32)
        start_y = (row_tile * TILE + halo - REACH + shift_y).astype(jnp.int32)
        start_x = (col_tile * TILE_W + halo - REACH + shift_x).astype(jnp.int32)
        window = lax.dynamic_slice(padded, (start_y, zero, start_x), (TILE + 2 * REACH, chans, TILE_W + 2 * REACH)).astype(jnp.float32)
        blocks = []
        for lift in range(span):
            for slide in range(span):
                slab = window[lift:lift + TILE, :, slide:slide + TILE_W]
                blocks.append(lax.optimization_barrier(jnp.sum(here * slab, axis=1)))
        return jnp.stack(blocks, axis=1)
    row_ids = jnp.arange(shifts.shape[0], dtype=jnp.int32)
    col_ids = jnp.arange(shifts.shape[1], dtype=jnp.int32)
    result = jax.vmap(lambda r: jax.vmap(lambda c: one_tile(r, c))(col_ids))(row_ids)
    result = (result * (1.0 / math.sqrt(CF))).astype(jnp.bfloat16)
    count_y, count_x = (shifts.shape[0], shifts.shape[1])
    result = jnp.transpose(result, (0, 2, 3, 1, 4))
    return result.reshape(count_y * TILE, span * span, count_x * TILE_W)

def reference(sections, tile_shift, w_first, w_second, w_third, w_fourth, w_fifth):
    features = lax.map(lambda one: encode(one, w_first, w_second, w_third, w_fourth, w_fifth), sections)
    halo = REACH + BOUND
    prior = jnp.concatenate([jnp.zeros_like(features[:1]), features[:-1]], axis=0)
    source = jnp.pad(prior, ((0, 0), (halo, halo), (0, 0), (0, 0)))
    return lax.map(lambda packed: correlate(packed[0], packed[1], packed[2]), (features, source, tile_shift))
```

```python
import functools
import math

import jax
import jax.numpy as jnp
from jax import lax
from jax.experimental import pallas as pl
from jax.experimental.pallas import tpu as pltpu
from jax.sharding import PartitionSpec as P

REACH = 8
SPAN = 2 * REACH + 1
OFFSETS = SPAN * SPAN
BF = jnp.bfloat16
F32 = jnp.float32

ROWS = 256
CHUNK = 64
BASE = 120
SLACK = 536


def iota(shape, dim):
    return lax.broadcasted_iota(jnp.int32, shape, dim)


def dot(a, b):
    return jnp.dot(a, b, preferred_element_type=F32)


def expand_weights(w1, w2, w3, w4, w5, e1, e2, e3, e4, e5):
    pixel = iota((128, 128), 0)
    column = iota((128, 128), 1) // 32
    for k1 in range(2):
        wide = [
            jnp.broadcast_to(jnp.concatenate([w1[k1, kx].astype(F32)] * 4, axis=1), (128, 128))
            for kx in range(2)
        ]
        for g in range(16):
            phase = pixel - 2 * (4 * g + column)
            block = jnp.where(phase == 0, wide[0], jnp.where(phase == 1, wide[1], 0.0))
            e1[k1 * 128 : k1 * 128 + 128, g * 128 : g * 128 + 128] = block.astype(BF)

    def spread(pieces, rows, outs, count):
        bands = []
        for line in pieces:
            bands.append(
                jnp.concatenate(
                    [jnp.zeros((rows, outs), F32) if p is None else p for p in line], axis=1
                )
            )
        return jnp.concatenate(bands, axis=0).astype(BF)

    for k in range(2):
        pieces = [
            [w2[k, ci % 2].astype(F32) if ci // 2 == co else None for co in range(4)]
            for ci in range(8)
        ]
        e2[k] = spread(pieces, 32, 64, 4)
        pieces = [
            [w3[k, ci % 2].astype(F32) if ci // 2 == co else None for co in range(2)]
            for ci in range(4)
        ]
        e3[k] = spread(pieces, 64, 64, 2)
    e4[...] = spread(
        [[w4[...].astype(F32) if ci == co else None for co in range(4)] for ci in range(4)], 64, 64, 4
    )
    e5[...] = spread(
        [[w5[...].astype(F32) if ci == co else None for co in range(4)] for ci in range(4)], 64, 32, 4
    )


def relu(x):
    return jnp.maximum(x, 0.0).astype(BF)


def encode_chunk(chunk, px, xs, a1, a2, a3, e1, e2, e3, e4, e5, perm):
    for part in range(CHUNK // 32):
        start = pl.multiple_of((chunk * (CHUNK // 32) + part) * 256, 256)
        sorted_rows = dot(perm[...], px[pl.ds(start, 256), :]).astype(BF)
        for k in range(8):
            xs[k // 2, part * 32 : part * 32 + 32, (k % 2) * 128 : (k % 2) * 128 + 128] = sorted_rows[
                k * 32 : k * 32 + 32
            ]
    lhs = xs[...].reshape(4 * CHUNK, 256)
    for j in range(8):
        out = relu(dot(lhs, e1[:, 256 * j : 256 * j + 256]))
        out = out.reshape(2, 2, CHUNK, 256)
        a1[0, j] = out[:, 0].reshape(2 * CHUNK, 256)
        a1[1, j] = out[:, 1].reshape(2 * CHUNK, 256)
    for jj in range(2):
        l0 = a1[0, 4 * jj : 4 * jj + 4].reshape(8 * CHUNK, 256)
        l1 = a1[1, 4 * jj : 4 * jj + 4].reshape(8 * CHUNK, 256)
        out = relu(dot(l0, e2[0]) + dot(l1, e2[1])).reshape(4, 2, CHUNK, 256)
        a2[0, 4 * jj : 4 * jj + 4] = out[:, 0]
        a2[1, 4 * jj : 4 * jj + 4] = out[:, 1]
    l0 = a2[0].reshape(8 * CHUNK, 256)
    l1 = a2[1].reshape(8 * CHUNK, 256)
    out = relu(dot(l0, e3[0]) + dot(l1, e3[1])).reshape(4, 2, CHUNK, 128)
    a3[:, :, 0:128] = out[:, 0]
    a3[:, :, 128:256] = out[:, 1]
    out = relu(dot(a3[...].reshape(4 * CHUNK, 256), e4[...]))
    return dot(out, e5[...]).astype(BF).reshape(4, CHUNK, 128)


def encoder_kernel(px, w1, w2, w3, w4, w5, out, xs, a1, a2, a3, e1, e2, e3, e4, e5, perm):
    expand_weights(w1, w2, w3, w4, w5, e1, e2, e3, e4, e5)
    r = iota((256, 256), 0)
    c = iota((256, 256), 1)
    perm[...] = jnp.where(8 * (r % 32) + r // 32 == c, 1.0, 0.0).astype(BF)

    @pl.loop(0, ROWS // CHUNK)
    def _(chunk):
        done = encode_chunk(chunk, px.at[0], xs, a1, a2, a3, e1, e2, e3, e4, e5, perm)
        out[:, pl.ds(pl.multiple_of(chunk * CHUNK, CHUNK), CHUNK), :] = done


def encode(sections, weights):
    vmem = pl.BlockSpec(memory_space=pltpu.VMEM)
    return pl.pallas_call(
        encoder_kernel,
        out_shape=jax.ShapeDtypeStruct((4, ROWS, 128), BF),
        in_specs=[vmem] * 6,
        out_specs=vmem,
        scratch_shapes=[
            pltpu.VMEM((4, CHUNK, 256), BF),
            pltpu.VMEM((2, 8, 2 * CHUNK, 256), BF),
            pltpu.VMEM((2, 8, CHUNK, 256), BF),
            pltpu.VMEM((4, CHUNK, 256), BF),
            pltpu.VMEM((256, 2048), BF),
            pltpu.VMEM((2, 256, 256), BF),
            pltpu.VMEM((2, 256, 128), BF),
            pltpu.VMEM((256, 256), BF),
            pltpu.VMEM((256, 128), BF),
            pltpu.VMEM((256, 256), BF),
        ],
        compiler_params=pltpu.CompilerParams(vmem_limit_bytes=48 * 2**20),
        name="encode",
    )(sections, *weights)


def correlate_kernel(shift, cur, prior, out, cur32, wide, lhs, rhs, picked, rows):
    wide[0:4] = jnp.zeros((4, 48, 128), F32)
    wide[68:72] = jnp.zeros((4, 48, 128), F32)

    @pl.loop(0, 16)
    def _(i):
        wide[pl.ds(4 + 4 * i, 4)] = prior[pl.ds(4 * i, 4)].astype(F32)
        cur32[pl.ds(4 * i, 4)] = cur[pl.ds(4 * i, 4)].astype(F32)

    lane = iota((8, 128), 1)
    slot = lane // 32
    sub = iota((8, 128), 0)
    lane256 = iota((8, 256), 1)
    block = (lane256 % 32) // 8

    for side in range(2):
        for j in range(4):
            tile = 2 * side + j // 2
            dy = shift[0, 0, tile, 0]
            dx = shift[0, 0, tile, 1]
            if j % 2 == 0:
                @pl.loop(0, 23)
                def _(q):
                    here = wide[16 * tile + q, pl.ds(8 + dy, 32), :]
                    beside = wide[16 * tile + q + 1, pl.ds(8 + dy, 32), :]
                    lhs[0, q] = here.astype(BF)
                    for e in range(1, 4):
                        mixed = jnp.where(iota((32, 128), 1) < 32 * e, beside, here)
                        lhs[e, q] = pltpu.roll(mixed, 128 - 32 * e, 1).astype(BF)

            for half in range(2):
                for u in range(8):
                    y = 8 * half + (u % 4 - j) % 4 + 4 * (u // 4)
                    for m in range(4):
                        q = 32 * side + 8 * j + 2 * m
                        a = jnp.broadcast_to(cur32[q, y : y + 1, :], (8, 128))
                        b = jnp.broadcast_to(cur32[q + 1, y : y + 1, :], (8, 128))
                        a = jnp.where(slot == sub, a, 0.0)
                        b = jnp.where(slot + 4 == sub, b, 0.0)
                        rhs[u * 32 + 8 * m : u * 32 + 8 * m + 8, 0:128] = a
                        rhs[u * 32 + 8 * m : u * 32 + 8 * m + 8, 128:256] = b
                weights = rhs[...].astype(BF)
                for jj in range(8):
                    count = 6 if jj == 0 else 5
                    place = 8 + dx + 32 * (j % 2) + jj
                    e = lax.rem(place, 4)
                    q = lax.div(place, 4)
                    parts = [
                        jnp.concatenate([lhs[e, q + 2 * m], lhs[e, q + 2 * m + 1]], axis=1)
                        for m in range(count)
                    ]
                    product = lax.dot_general(
                        jnp.concatenate(parts, axis=0),
                        weights,
                        (((1,), (1,)), ((), ())),
                        preferred_element_type=F32,
                    ).reshape(count, 4, 8, 256)
                    for ox in range(jj, SPAN, 8):
                        m = ox // 8
                        for i in range(3):
                            piece = product[m + 3, i + half]
                            for b in (2, 1, 0):
                                piece = jnp.where(block == b, product[m + b, i + half], piece)
                            picked[half, j, ox, i] = piece

        for half in range(2):
            @pl.loop(0, SPAN)
            def _(ox):
                for v in range(2):
                    for i in range(3):
                        blocks = [picked[half, j, ox, i, :, 128 * v : 128 * v + 128] for j in range(4)]
                        for k in range(4):
                            merged = blocks[(3 - k) % 4]
                            for u in (2, 1, 0):
                                merged = jnp.where(slot == u, blocks[(u - k) % 4], merged)
                            if k:
                                merged = pltpu.roll(merged, 128 - 32 * k, 1)
                            start = BASE + (8 * i - 4 * v - k) * SPAN + ox
                            rows[4 * v + k, pl.ds(start, 8, stride=SPAN), :] = merged

            @pl.loop(0, 8)
            def _(y):
                done = rows[y, BASE : BASE + OFFSETS, :] * (1.0 / math.sqrt(32))
                out[0, 8 * half + y, :, 128 * side : 128 * side + 128] = done.astype(BF)


def correlate(current, prior, tile_shift):
    vmem = pl.BlockSpec(memory_space=pltpu.VMEM)
    return pl.pallas_call(
        correlate_kernel,
        out_shape=jax.ShapeDtypeStruct((1, 16, OFFSETS, 256), BF),
        in_specs=[pl.BlockSpec(memory_space=pltpu.SMEM), vmem, vmem],
        out_specs=vmem,
        scratch_shapes=[
            pltpu.VMEM((64, 16, 128), F32),
            pltpu.VMEM((72, 48, 128), F32),
            pltpu.VMEM((4, 24, 32, 128), BF),
            pltpu.VMEM((256, 256), F32),
            pltpu.VMEM((2, 4, SPAN, 3, 8, 256), F32),
            pltpu.VMEM((8, SLACK, 128), F32),
        ],
        compiler_params=pltpu.CompilerParams(vmem_limit_bytes=48 * 2**20),
        name="correlate",
    )(tile_shift, current, prior)


def shifted(block, axis, distance):
    devices = range(lax.axis_size(axis))
    route = [(i - distance, i) for i in devices if i - distance in devices]
    return lax.ppermute(block, axis, route)


def local(sections, tile_shift, w_first, w_second, w_third, w_fourth, w_fifth):
    weights = (w_first, w_second, w_third, w_fourth, w_fifth)
    bands = encode(sections, weights)
    current = lax.all_to_all(bands, "tile", split_axis=1, concat_axis=0, tiled=True)
    before = shifted(current, "sec", 1)
    prior = jnp.concatenate([shifted(before, "tile", 1), before, shifted(before, "tile", -1)], axis=1)
    return correlate(current, prior, tile_shift)


def solution(mesh):
    placed = (P("sec", None, "tile"), P("sec", "tile", None, None), P(), P(), P(), P(), P())
    return jax.shard_map(
        local, mesh=mesh, in_specs=placed, out_specs=P("sec", "tile", None, None), check_vma=False
    )
```

```python
import functools
import math

import jax
import jax.numpy as jnp
from jax import lax
from jax.experimental import pallas as pl
from jax.experimental.pallas import tpu as pltpu
from jax.sharding import PartitionSpec as P

REACH = 8
SPAN = 2 * REACH + 1
OFFSETS = SPAN * SPAN
BF = jnp.bfloat16
F32 = jnp.float32

ROWS = 256
CHUNK = 64
BASE = 7


def iota(shape, dim):
    return lax.broadcasted_iota(jnp.int32, shape, dim)


def dot(a, b):
    return jnp.dot(a, b, preferred_element_type=F32)


def expand_weights(w1, w2, w3, w4, w5, e1, e2, e3, e4, e5):
    pixel = iota((128, 128), 0)
    column = iota((128, 128), 1) // 32
    for k1 in range(2):
        wide = [
            jnp.broadcast_to(jnp.concatenate([w1[k1, kx : kx + 1].astype(F32)] * 4, axis=1), (128, 128))
            for kx in range(2)
        ]
        for g in range(16):
            phase = pixel - 2 * (4 * g + column)
            block = jnp.where(phase == 0, wide[0], jnp.where(phase == 1, wide[1], 0.0))
            e1[k1 * 128 : k1 * 128 + 128, g * 128 : g * 128 + 128] = block.astype(BF)

    def spread(pieces, rows, outs, count):
        bands = []
        for line in pieces:
            bands.append(
                jnp.concatenate(
                    [jnp.zeros((rows, outs), F32) if p is None else p for p in line], axis=1
                )
            )
        return jnp.concatenate(bands, axis=0).astype(BF)

    for k in range(2):
        pieces = [
            [w2[k, ci % 2].astype(F32) if ci // 2 == co else None for co in range(4)]
            for ci in range(8)
        ]
        e2[k] = spread(pieces, 32, 64, 4)
        pieces = [
            [w3[k, ci % 2].astype(F32) if ci // 2 == co else None for co in range(2)]
            for ci in range(4)
        ]
        e3[k] = spread(pieces, 64, 64, 2)
    e4[...] = spread(
        [[w4[...].astype(F32) if ci == co else None for co in range(4)] for ci in range(4)], 64, 64, 4
    )
    e5[...] = spread(
        [[jnp.transpose(w5[...].astype(F32)) if ci == co else None for co in range(4)] for ci in range(4)], 64, 32, 4
    )


def relu(x):
    return jnp.maximum(x, 0.0).astype(BF)


def encode_chunk(chunk, px, xs, a1, a2, a3, e1, e2, e3, e4, e5, perm):
    for part in range(CHUNK // 32):
        start = pl.multiple_of((chunk * (CHUNK // 32) + part) * 256, 256)
        sorted_rows = dot(perm[...], px[pl.ds(start, 256), :]).astype(BF)
        for k in range(8):
            xs[k // 2, part * 32 : part * 32 + 32, (k % 2) * 128 : (k % 2) * 128 + 128] = sorted_rows[
                k * 32 : k * 32 + 32
            ]
    lhs = xs[...].reshape(4 * CHUNK, 256)
    for j in range(8):
        out = relu(dot(lhs, e1[:, 256 * j : 256 * j + 256]))
        out = out.reshape(2, 2, CHUNK, 256)
        a1[0, j] = out[:, 0].reshape(2 * CHUNK, 256)
        a1[1, j] = out[:, 1].reshape(2 * CHUNK, 256)
    for jj in range(2):
        l0 = a1[0, 4 * jj : 4 * jj + 4].reshape(8 * CHUNK, 256)
        l1 = a1[1, 4 * jj : 4 * jj + 4].reshape(8 * CHUNK, 256)
        out = relu(dot(l0, e2[0]) + dot(l1, e2[1])).reshape(4, 2, CHUNK, 256)
        a2[0, 4 * jj : 4 * jj + 4] = out[:, 0]
        a2[1, 4 * jj : 4 * jj + 4] = out[:, 1]
    l0 = a2[0].reshape(8 * CHUNK, 256)
    l1 = a2[1].reshape(8 * CHUNK, 256)
    out = relu(dot(l0, e3[0]) + dot(l1, e3[1])).reshape(4, 2, CHUNK, 128)
    a3[:, :, 0:128] = out[:, 0]
    a3[:, :, 128:256] = out[:, 1]
    out = relu(dot(a3[...].reshape(4 * CHUNK, 256), e4[...]))
    return dot(out, e5[...]).astype(BF).reshape(4, CHUNK, 128)


def encoder_kernel(px, w1, w2, w3, w4, w5, out, xs, a1, a2, a3, e1, e2, e3, e4, e5, perm):
    expand_weights(w1, w2, w3, w4, w5, e1, e2, e3, e4, e5)
    r = iota((256, 256), 0)
    c = iota((256, 256), 1)
    perm[...] = jnp.where(8 * (r % 32) + r // 32 == c, 1.0, 0.0).astype(BF)

    @pl.loop(0, ROWS // CHUNK)
    def _(chunk):
        done = encode_chunk(chunk, px.at[0], xs, a1, a2, a3, e1, e2, e3, e4, e5, perm)
        out[:, pl.ds(pl.multiple_of(chunk * CHUNK, CHUNK), CHUNK), :] = done


def encode(sections, weights):
    vmem = pl.BlockSpec(memory_space=pltpu.VMEM)
    return pl.pallas_call(
        encoder_kernel,
        out_shape=jax.ShapeDtypeStruct((4, ROWS, 128), BF),
        in_specs=[vmem] * 6,
        out_specs=vmem,
        scratch_shapes=[
            pltpu.VMEM((4, CHUNK, 256), BF),
            pltpu.VMEM((2, 8, 2 * CHUNK, 256), BF),
            pltpu.VMEM((2, 8, CHUNK, 256), BF),
            pltpu.VMEM((4, CHUNK, 256), BF),
            pltpu.VMEM((256, 2048), BF),
            pltpu.VMEM((2, 256, 256), BF),
            pltpu.VMEM((2, 256, 128), BF),
            pltpu.VMEM((256, 256), BF),
            pltpu.VMEM((256, 128), BF),
            pltpu.VMEM((256, 256), BF),
        ],
        compiler_params=pltpu.CompilerParams(vmem_limit_bytes=48 * 2**20),
        name="encode",
    )(sections, *weights)


def correlate_kernel(shift, cur, prior, out, cur32, wide, lhs, rhs, picked, rows):
    wide[0:4] = jnp.zeros((4, 48, 128), F32)
    wide[68:72] = jnp.zeros((4, 48, 128), F32)

    @pl.loop(0, 16)
    def _(i):
        wide[pl.ds(4 + 4 * i, 4)] = prior[pl.ds(4 * i, 4)].astype(F32)
        cur32[pl.ds(4 * i, 4)] = cur[pl.ds(4 * i, 4)].astype(F32)

    lane = iota((8, 128), 1)
    slot = lane // 32
    sub = iota((8, 128), 0)
    lane256 = iota((8, 256), 1)
    block = (lane256 % 32) // 8

    for side in range(2):
        for j in range(4):
            tile = 2 * side + j // 2
            dy = shift[0, tile]
            dx = shift[1, tile]
            if j % 2 == 0:
                @pl.loop(0, 23)
                def _(q):
                    here = wide[16 * tile + q, pl.ds(8 + dy, 32), :]
                    beside = wide[16 * tile + q + 1, pl.ds(8 + dy, 32), :]
                    lhs[0, q] = here.astype(BF)
                    for e in range(1, 4):
                        mixed = jnp.where(iota((32, 128), 1) < 32 * e, beside, here)
                        lhs[e, q] = pltpu.roll(mixed, 128 - 32 * e, 1).astype(BF)

            for half in range(2):
                for u in range(8):
                    y = 8 * half + (u % 4 - j) % 4 + 4 * (u // 4)
                    for m in range(4):
                        q = 32 * side + 8 * j + 2 * m
                        a = jnp.broadcast_to(cur32[q, y : y + 1, :], (8, 128))
                        b = jnp.broadcast_to(cur32[q + 1, y : y + 1, :], (8, 128))
                        a = jnp.where(slot == sub, a, 0.0)
                        b = jnp.where(slot + 4 == sub, b, 0.0)
                        rhs[u * 32 + 8 * m : u * 32 + 8 * m + 8, 0:128] = a
                        rhs[u * 32 + 8 * m : u * 32 + 8 * m + 8, 128:256] = b
                weights = rhs[...].astype(BF)
                for jj in range(8):
                    count = 6 if jj == 0 else 5
                    place = 8 + dx + 32 * (j % 2) + jj
                    e = lax.rem(place, 4)
                    q = lax.div(place, 4)
                    parts = [
                        jnp.concatenate([lhs[e, q + 2 * m], lhs[e, q + 2 * m + 1]], axis=1)
                        for m in range(count)
                    ]
                    product = lax.dot_general(
                        jnp.concatenate(parts, axis=0),
                        weights,
                        (((1,), (1,)), ((), ())),
                        preferred_element_type=F32,
                    ).reshape(count, 4, 8, 256)
                    for ox in range(jj, SPAN, 8):
                        m = ox // 8
                        for i in range(3):
                            piece = product[m + 3, i + half]
                            for b in (2, 1, 0):
                                piece = jnp.where(block == b, product[m + b, i + half], piece)
                            picked[half, j, ox, i] = piece

        for half in range(2):
            @pl.loop(0, SPAN)
            def _(ox):
                for v in range(2):
                    for i in range(3):
                        blocks = [picked[half, j, ox, i, :, 128 * v : 128 * v + 128] for j in range(4)]
                        for k in range(4):
                            merged = blocks[(3 - k) % 4]
                            for u in (2, 1, 0):
                                merged = jnp.where(slot == u, blocks[(u - k) % 4], merged)
                            if k:
                                merged = pltpu.roll(merged, 128 - 32 * k, 1)
                            y = 4 * v + k
                            start = ((BASE + 8 * i - y) * SPAN + ox) * 8 + y
                            rows[pl.ds(start, 8, stride=8 * SPAN), :] = merged

            @pl.loop(0, SPAN)
            def _(oy):
                start = pl.multiple_of((BASE + oy) * SPAN * 8, 8)
                done = rows[pl.ds(start, SPAN * 8), :] * (1.0 / math.sqrt(32))
                done = done.astype(BF).reshape(SPAN, 8, 128)
                out[pl.ds(oy * SPAN, SPAN), 8 * half : 8 * half + 8, 128 * side : 128 * side + 128] = done


def correlate(current, prior, tile_shift):
    vmem = pl.BlockSpec(memory_space=pltpu.VMEM)
    return pl.pallas_call(
        correlate_kernel,
        out_shape=jax.ShapeDtypeStruct((OFFSETS, 16, 256), BF),
        in_specs=[pl.BlockSpec(memory_space=pltpu.SMEM), vmem, vmem],
        out_specs=vmem,
        scratch_shapes=[
            pltpu.VMEM((64, 16, 128), F32),
            pltpu.VMEM((72, 48, 128), F32),
            pltpu.VMEM((4, 24, 32, 128), BF),
            pltpu.VMEM((256, 256), F32),
            pltpu.VMEM((2, 4, SPAN, 3, 8, 256), F32),
            pltpu.VMEM(((BASE + 24) * SPAN * 8, 128), F32),
        ],
        compiler_params=pltpu.CompilerParams(vmem_limit_bytes=48 * 2**20),
        name="correlate",
    )(tile_shift, current, prior)


def exchange_kernel(bands, cur, prior, send_sem, cur_sem, prior_sem, halo_sem, local_sem):
    s = lax.axis_index("sec")
    t = lax.axis_index("tile")
    secs = lax.axis_size("sec")
    tiles = lax.axis_size("tile")
    barrier = pltpu.get_barrier_semaphore()

    def greet(to_s, to_t):
        pl.semaphore_signal(
            barrier, inc=1, device_id=(to_s, to_t), device_id_type=pl.DeviceIdType.MESH
        )

    @pl.loop(1, tiles)
    def _(k):
        greet(s, lax.rem(t + k, tiles))

    @pl.when(s > 0)
    def _():
        @pl.loop(0, tiles)
        def _(k):
            greet(s - 1, lax.rem(t + k, tiles))

    home = pltpu.make_async_copy(
        bands.at[:, pl.ds(pl.multiple_of(16 * t, 16), 16)], cur.at[pl.ds(4 * t, 4)], local_sem
    )
    home.start()
    blank = jnp.zeros((64, 16, 128), BF)

    @pl.when((s == 0) | (t == 0))
    def _():
        prior[:, 0:16] = blank

    @pl.when((s == 0) | (t == tiles - 1))
    def _():
        prior[:, 32:48] = blank

    @pl.when(s == 0)
    def _():
        prior[:, 16:32] = blank

    @pl.when(s < secs - 1)
    def _():
        pl.semaphore_wait(barrier, 2 * tiles - 1)

    @pl.when(s == secs - 1)
    def _():
        pl.semaphore_wait(barrier, tiles - 1)

    def block_of(to_t):
        return bands.at[:, pl.ds(pl.multiple_of(16 * to_t, 16), 16)]

    @pl.loop(0, tiles)
    def _(k):
        to_t = lax.rem(t + k, tiles)

        @pl.when(s < secs - 1)
        def _():
            pltpu.make_async_remote_copy(
                src_ref=block_of(to_t),
                dst_ref=prior.at[pl.ds(4 * t, 4), 16:32],
                send_sem=send_sem.at[0],
                recv_sem=prior_sem,
                device_id=(s + 1, to_t),
                device_id_type=pl.DeviceIdType.MESH,
            ).start()

        @pl.when(k > 0)
        def _():
            pltpu.make_async_remote_copy(
                src_ref=block_of(to_t),
                dst_ref=cur.at[pl.ds(4 * t, 4)],
                send_sem=send_sem.at[1],
                recv_sem=cur_sem,
                device_id=(s, to_t),
                device_id_type=pl.DeviceIdType.MESH,
            ).start()

    def halo(to_t, row, sem):
        return pltpu.make_async_remote_copy(
            src_ref=prior.at[:, 16:32],
            dst_ref=prior.at[:, row : row + 16],
            send_sem=send_sem.at[2 + sem],
            recv_sem=halo_sem.at[sem],
            device_id=(s, to_t),
            device_id_type=pl.DeviceIdType.MESH,
        )

    def arrive(ref, sem):
        pltpu.make_async_copy(ref, ref, sem).wait()

    @pl.when(s > 0)
    def _():
        arrive(prior.at[:, 16:32], prior_sem)

        @pl.when(t < tiles - 1)
        def _():
            halo(t + 1, 0, 0).start()

        @pl.when(t > 0)
        def _():
            halo(t - 1, 32, 1).start()

    arrive(cur.at[0:60], cur_sem)
    home.wait()
    arrive(bands.at[:, 0:240], send_sem.at[1])

    @pl.when(s < secs - 1)
    def _():
        arrive(bands, send_sem.at[0])

    @pl.when(s > 0)
    def _():
        @pl.when(t < tiles - 1)
        def _():
            halo(t + 1, 0, 0).wait_send()
            arrive(prior.at[:, 32:48], halo_sem.at[1])

        @pl.when(t > 0)
        def _():
            halo(t - 1, 32, 1).wait_send()
            arrive(prior.at[:, 0:16], halo_sem.at[0])


def exchange(bands):
    vmem = pl.BlockSpec(memory_space=pltpu.VMEM)
    return pl.pallas_call(
        exchange_kernel,
        out_shape=(
            jax.ShapeDtypeStruct((64, 16, 128), BF),
            jax.ShapeDtypeStruct((64, 48, 128), BF),
        ),
        in_specs=[vmem],
        out_specs=(vmem, vmem),
        scratch_shapes=[
            pltpu.SemaphoreType.DMA((4,)),
            pltpu.SemaphoreType.DMA,
            pltpu.SemaphoreType.DMA,
            pltpu.SemaphoreType.DMA((2,)),
            pltpu.SemaphoreType.DMA,
        ],
        compiler_params=pltpu.CompilerParams(collective_id=0, has_side_effects=True),
        name="exchange",
    )(bands)


def local(sections, tile_shift, w_first, w_second, w_third, w_fourth, w_fifth):
    weights = (w_first.reshape(2, 2, 32), w_second, w_third, w_fourth, w_fifth.T)
    bands = encode(sections, weights)
    current, prior = exchange(bands)
    shift = jnp.transpose(tile_shift, (0, 1, 3, 2)).reshape(2, 4)
    found = correlate(current, prior, shift)
    return jnp.transpose(found[None], (0, 2, 1, 3))


def solution(mesh):
    placed = (P("sec", None, "tile"), P("sec", "tile", None, None), P(), P(), P(), P(), P())
    return jax.shard_map(
        local, mesh=mesh, in_specs=placed, out_specs=P("sec", "tile", None, None), check_vma=False
    )
```

```python
import functools
import math

import jax
import jax.numpy as jnp
from jax import lax
from jax.experimental import pallas as pl
from jax.experimental.pallas import tpu as pltpu
from jax.sharding import PartitionSpec as P

REACH = 8
SPAN = 2 * REACH + 1
OFFSETS = SPAN * SPAN
BF = jnp.bfloat16
F32 = jnp.float32

ROWS = 256
CHUNK = 64
LIMIT = 60 * 2**20
BASE = 7


def iota(shape, dim):
    return lax.broadcasted_iota(jnp.int32, shape, dim)


def dot(a, b):
    return jnp.dot(a, b, preferred_element_type=F32)


def expand_weights(w1, w2, w3, w4, w5, e1, e2, e3, e4, e5):
    pixel = iota((128, 128), 0)
    column = iota((128, 128), 1) // 32
    for k1 in range(2):
        wide = [
            jnp.broadcast_to(jnp.concatenate([w1[k1, kx : kx + 1].astype(F32)] * 4, axis=1), (128, 128))
            for kx in range(2)
        ]
        for g in range(16):
            phase = pixel - 2 * (4 * g + column)
            block = jnp.where(phase == 0, wide[0], jnp.where(phase == 1, wide[1], 0.0))
            e1[k1 * 128 : k1 * 128 + 128, g * 128 : g * 128 + 128] = block.astype(BF)

    def spread(pieces, rows, outs, count):
        bands = []
        for line in pieces:
            bands.append(
                jnp.concatenate(
                    [jnp.zeros((rows, outs), F32) if p is None else p for p in line], axis=1
                )
            )
        return jnp.concatenate(bands, axis=0).astype(BF)

    for k in range(2):
        pieces = [
            [w2[k, ci % 2].astype(F32) if ci // 2 == co else None for co in range(4)]
            for ci in range(8)
        ]
        e2[k] = spread(pieces, 32, 64, 4)
        pieces = [
            [w3[k, ci % 2].astype(F32) if ci // 2 == co else None for co in range(2)]
            for ci in range(4)
        ]
        e3[k] = spread(pieces, 64, 64, 2)
    e4[...] = spread(
        [[w4[...].astype(F32) if ci == co else None for co in range(4)] for ci in range(4)], 64, 64, 4
    )
    e5[...] = spread(
        [[jnp.transpose(w5[...].astype(F32)) if ci == co else None for co in range(4)] for ci in range(4)], 64, 32, 4
    )


def relu(x):
    return jnp.maximum(x, 0.0).astype(BF)


def encode_chunk(px, xs, a1, a2, a3, e1, e2, e3, e4, e5, perm):
    for part in range(CHUNK // 32):
        sorted_rows = dot(perm[...], px[part * 256 : part * 256 + 256, :]).astype(BF)
        for k in range(8):
            xs[k // 2, part * 32 : part * 32 + 32, (k % 2) * 128 : (k % 2) * 128 + 128] = sorted_rows[
                k * 32 : k * 32 + 32
            ]
    lhs = xs[...].reshape(4 * CHUNK, 256)
    for j in range(8):
        out = relu(dot(lhs, e1[:, 256 * j : 256 * j + 256]))
        out = out.reshape(2, 2, CHUNK, 256)
        a1[0, j] = out[:, 0].reshape(2 * CHUNK, 256)
        a1[1, j] = out[:, 1].reshape(2 * CHUNK, 256)
    for jj in range(2):
        l0 = a1[0, 4 * jj : 4 * jj + 4].reshape(8 * CHUNK, 256)
        l1 = a1[1, 4 * jj : 4 * jj + 4].reshape(8 * CHUNK, 256)
        out = relu(dot(l0, e2[0]) + dot(l1, e2[1])).reshape(4, 2, CHUNK, 256)
        a2[0, 4 * jj : 4 * jj + 4] = out[:, 0]
        a2[1, 4 * jj : 4 * jj + 4] = out[:, 1]
    l0 = a2[0].reshape(8 * CHUNK, 256)
    l1 = a2[1].reshape(8 * CHUNK, 256)
    out = relu(dot(l0, e3[0]) + dot(l1, e3[1])).reshape(4, 2, CHUNK, 128)
    a3[:, :, 0:128] = out[:, 0]
    a3[:, :, 128:256] = out[:, 1]
    out = relu(dot(a3[...].reshape(4 * CHUNK, 256), e4[...]))
    return dot(out, e5[...]).astype(BF).reshape(4, CHUNK, 128)


def share_kernel(
    px_hbm, w1_hbm, w2_hbm, w3_hbm, w4_hbm, w5_hbm, cur, prior,
    px, w1, w2, w3, w4, w5, bands, xs, a1, a2, a3, e1, e2, e3, e4, e5, perm,
    load_sem, px_sem, send_sem, cur_sem, prior_sem, halo_send, halo_recv, home_sem,
):
    s = lax.axis_index("sec")
    t = lax.axis_index("tile")
    secs = lax.axis_size("sec")
    tiles = lax.axis_size("tile")
    group = lax.rem(t, 4)
    member = lax.div(t, 4)
    chunks = ROWS // CHUNK
    pixels = 8 * CHUNK

    loads = [
        pltpu.make_async_copy(a, b, load_sem.at[i])
        for i, (a, b) in enumerate(
            [(w1_hbm, w1), (w2_hbm, w2), (w3_hbm, w3), (w4_hbm, w4), (w5_hbm, w5)]
        )
    ]
    for load in loads:
        load.start()

    def fetch(phase):
        chunk = lax.rem(t + phase, chunks)
        return pltpu.make_async_copy(
            px_hbm.at[0, pl.ds(pl.multiple_of(chunk * pixels, pixels), pixels)],
            px.at[phase],
            px_sem.at[phase],
        )

    for phase in range(chunks):
        fetch(phase).start()

    barrier = pltpu.get_barrier_semaphore()

    def greet(to_s, to_t):
        pl.semaphore_signal(
            barrier, inc=1, device_id=(to_s, to_t), device_id_type=pl.DeviceIdType.MESH
        )

    @pl.loop(1, tiles)
    def _(k):
        greet(s, lax.rem(t + k, tiles))

    @pl.when(s > 0)
    def _():
        @pl.loop(0, tiles)
        def _(k):
            greet(s - 1, lax.rem(t + k, tiles))

    r = iota((256, 256), 0)
    c = iota((256, 256), 1)
    perm[...] = jnp.where(8 * (r % 32) + r // 32 == c, 1.0, 0.0).astype(BF)
    for load in loads:
        load.wait()
    expand_weights(w1, w2, w3, w4, w5, e1, e2, e3, e4, e5)

    def band_of(to_t):
        return bands.at[:, pl.ds(pl.multiple_of(16 * to_t, 16), 16)]

    home = pltpu.make_async_copy(band_of(t), cur.at[member, group], home_sem)

    @pl.loop(0, chunks)
    def _(phase):
        chunk = lax.rem(t + phase, chunks)
        fetch(phase).wait()
        done = encode_chunk(px.at[phase], xs, a1, a2, a3, e1, e2, e3, e4, e5, perm)
        bands[:, pl.ds(pl.multiple_of(chunk * CHUNK, CHUNK), CHUNK), :] = done

        @pl.when(phase == 0)
        def _():
            @pl.when(s < secs - 1)
            def _():
                pl.semaphore_wait(barrier, 2 * tiles - 1)

            @pl.when(s == secs - 1)
            def _():
                pl.semaphore_wait(barrier, tiles - 1)

        @pl.loop(0, CHUNK // 16)
        def _(k):
            to_t = chunk * (CHUNK // 16) + lax.rem(k + member, CHUNK // 16)

            @pl.when(s < secs - 1)
            def _():
                pltpu.make_async_remote_copy(
                    src_ref=band_of(to_t),
                    dst_ref=prior.at[member, group, :, 16:32],
                    send_sem=send_sem.at[0],
                    recv_sem=prior_sem.at[group],
                    device_id=(s + 1, to_t),
                    device_id_type=pl.DeviceIdType.MESH,
                ).start()

            @pl.when(to_t != t)
            def _():
                pltpu.make_async_remote_copy(
                    src_ref=band_of(to_t),
                    dst_ref=cur.at[member, group],
                    send_sem=send_sem.at[1],
                    recv_sem=cur_sem.at[0],
                    device_id=(s, to_t),
                    device_id_type=pl.DeviceIdType.MESH,
                ).start()

            @pl.when(to_t == t)
            def _():
                home.start()

    def halo(to_t, row, side, g):
        return pltpu.make_async_remote_copy(
            src_ref=prior.at[:, g, :, 16:32],
            dst_ref=prior.at[:, g, :, row : row + 16],
            send_sem=halo_send.at[side, g],
            recv_sem=halo_recv.at[side, g],
            device_id=(s, to_t),
            device_id_type=pl.DeviceIdType.MESH,
        )

    def arrive(ref, sem):
        pltpu.make_async_copy(ref, ref, sem).wait()

    @pl.when(s > 0)
    def _():
        @pl.loop(0, 4)
        def _(k):
            g = lax.rem(member - k + 4, 4)
            arrive(prior.at[:, g, :, 16:32], prior_sem.at[g])

            @pl.when(t < tiles - 1)
            def _():
                halo(t + 1, 0, 0, g).start()

            @pl.when(t > 0)
            def _():
                halo(t - 1, 32, 1, g).start()

    home.wait()
    arrive(bands.at[:, 0:240], cur_sem.at[0])
    arrive(bands.at[:, 0:240], send_sem.at[1])

    @pl.when(s < secs - 1)
    def _():
        arrive(bands, send_sem.at[0])

    @pl.when(s > 0)
    def _():
        @pl.loop(0, 4)
        def _(g):
            @pl.when(t < tiles - 1)
            def _():
                halo(t + 1, 0, 0, g).wait_send()
                arrive(prior.at[:, g, :, 32:48], halo_recv.at[1, g])

            @pl.when(t > 0)
            def _():
                halo(t - 1, 32, 1, g).wait_send()
                arrive(prior.at[:, g, :, 0:16], halo_recv.at[0, g])


def share(sections, weights):
    hbm = pl.BlockSpec(memory_space=pltpu.HBM)
    return pl.pallas_call(
        share_kernel,
        out_shape=(
            jax.ShapeDtypeStruct((4, 4, 4, 16, 128), BF),
            jax.ShapeDtypeStruct((4, 4, 4, 48, 128), BF),
        ),
        in_specs=[hbm] * 6,
        out_specs=(hbm, hbm),
        scratch_shapes=[
            pltpu.VMEM((ROWS // CHUNK, 8 * CHUNK, 128), BF),
            *[pltpu.VMEM(w.shape, BF) for w in weights],
            pltpu.VMEM((4, ROWS, 128), BF),
            pltpu.VMEM((4, CHUNK, 256), BF),
            pltpu.VMEM((2, 8, 2 * CHUNK, 256), BF),
            pltpu.VMEM((2, 8, CHUNK, 256), BF),
            pltpu.VMEM((4, CHUNK, 256), BF),
            pltpu.VMEM((256, 2048), BF),
            pltpu.VMEM((2, 256, 256), BF),
            pltpu.VMEM((2, 256, 128), BF),
            pltpu.VMEM((256, 256), BF),
            pltpu.VMEM((256, 128), BF),
            pltpu.VMEM((256, 256), BF),
            pltpu.SemaphoreType.DMA((5,)),
            pltpu.SemaphoreType.DMA((ROWS // CHUNK,)),
            pltpu.SemaphoreType.DMA((2,)),
            pltpu.SemaphoreType.DMA((1,)),
            pltpu.SemaphoreType.DMA((4,)),
            pltpu.SemaphoreType.DMA((2, 4)),
            pltpu.SemaphoreType.DMA((2, 4)),
            pltpu.SemaphoreType.DMA,
        ],
        compiler_params=pltpu.CompilerParams(
            vmem_limit_bytes=LIMIT, collective_id=0, has_side_effects=True
        ),
        name="share",
    )(sections, *weights)


def correlate_kernel(
    shift, cur_hbm, prior_hbm, out_hbm, cur, prior, cur32, wide, lhs, rhs, picked, rows, out, in_sem, out_sem
):
    s = lax.axis_index("sec")
    t = lax.axis_index("tile")
    loads = []
    for i in range(4):
        near = pl.ds(16 * i, 16)
        loads.append(
            (
                pltpu.make_async_copy(prior_hbm.at[near], prior.at[near], in_sem.at[0, i]),
                pltpu.make_async_copy(cur_hbm.at[near], cur.at[near], in_sem.at[1, i]),
            )
        )
    for pair in loads:
        for load in pair:
            load.start()
    wide[0:4] = jnp.zeros((4, 48, 128), F32)
    wide[68:72] = jnp.zeros((4, 48, 128), F32)

    row = iota((1, 48, 128), 1)
    first = jnp.where(t == 0, 16, 0)
    last = jnp.where(t == lax.axis_size("tile") - 1, 32, 48)
    last = jnp.where(s == 0, 0, last)
    inside = (row >= first) & (row < last)
    for i in range(16):
        if i % 4 == 0:
            for load in loads[i // 4]:
                load.wait()
        wide[4 + 4 * i : 8 + 4 * i] = jnp.where(inside, prior[4 * i : 4 * i + 4].astype(F32), 0.0)
        cur32[4 * i : 4 * i + 4] = cur[4 * i : 4 * i + 4].astype(F32)

    lane = iota((8, 128), 1)
    slot = lane // 32
    sub = iota((8, 128), 0)
    lane256 = iota((8, 256), 1)
    block = (lane256 % 32) // 8

    sends = []
    for side in range(2):
        for j in range(4):
            tile = 2 * side + j // 2
            dy = shift[0, tile]
            dx = shift[1, tile]
            if j % 2 == 0:
                @pl.loop(0, 23, unroll=True)
                def _(q):
                    here = wide[16 * tile + q, pl.ds(8 + dy, 32), :]
                    beside = wide[16 * tile + q + 1, pl.ds(8 + dy, 32), :]
                    lhs[0, q] = here.astype(BF)
                    for e in range(1, 4):
                        mixed = jnp.where(iota((32, 128), 1) < 32 * e, beside, here)
                        lhs[e, q] = pltpu.roll(mixed, 128 - 32 * e, 1).astype(BF)

            for half in range(2):
                for u in range(8):
                    y = 8 * half + (u % 4 - j) % 4 + 4 * (u // 4)
                    for m in range(4):
                        q = 32 * side + 8 * j + 2 * m
                        a = jnp.broadcast_to(cur32[q, y : y + 1, :], (8, 128))
                        b = jnp.broadcast_to(cur32[q + 1, y : y + 1, :], (8, 128))
                        a = jnp.where(slot == sub, a, 0.0)
                        b = jnp.where(slot + 4 == sub, b, 0.0)
                        rhs[u * 32 + 8 * m : u * 32 + 8 * m + 8, 0:128] = a
                        rhs[u * 32 + 8 * m : u * 32 + 8 * m + 8, 128:256] = b
                weights = rhs[...].astype(BF)
                for jj in range(8):
                    count = 6 if jj == 0 else 5
                    place = 8 + dx + 32 * (j % 2) + jj
                    e = lax.rem(place, 4)
                    q = lax.div(place, 4)
                    parts = [
                        jnp.concatenate([lhs[e, q + 2 * m], lhs[e, q + 2 * m + 1]], axis=1)
                        for m in range(count)
                    ]
                    product = lax.dot_general(
                        jnp.concatenate(parts, axis=0),
                        weights,
                        (((1,), (1,)), ((), ())),
                        preferred_element_type=F32,
                    ).reshape(count, 4, 8, 256)
                    for ox in range(jj, SPAN, 8):
                        m = ox // 8
                        for i in range(3):
                            piece = product[m + 3, i + half]
                            for b in (2, 1, 0):
                                piece = jnp.where(block == b, product[m + b, i + half], piece)
                            picked[half, j, ox, i] = piece

        for half in range(2):
            @pl.loop(0, SPAN, unroll=True)
            def _(ox):
                for v in range(2):
                    for i in range(3):
                        blocks = [picked[half, j, ox, i, :, 128 * v : 128 * v + 128] for j in range(4)]
                        for k in range(4):
                            merged = blocks[(3 - k) % 4]
                            for u in (2, 1, 0):
                                merged = jnp.where(slot == u, blocks[(u - k) % 4], merged)
                            if k:
                                merged = pltpu.roll(merged, 128 - 32 * k, 1)
                            y = 4 * v + k
                            start = ((BASE + 8 * i - y) * SPAN + ox) * 8 + y
                            rows[pl.ds(start, 8, stride=8 * SPAN), :] = merged

            @pl.loop(0, SPAN, unroll=True)
            def _(oy):
                start = pl.multiple_of((BASE + oy) * SPAN * 8, 8)
                done = rows[pl.ds(start, SPAN * 8), :] * (1.0 / math.sqrt(32))
                done = done.astype(BF).reshape(SPAN, 8, 128)
                out[side, pl.ds(oy * SPAN, SPAN), 8 * half : 8 * half + 8, :] = done

        sends.append(
            pltpu.make_async_copy(
                out.at[side], out_hbm.at[:, :, pl.ds(128 * side, 128)], out_sem.at[side]
            )
        )
        sends[-1].start()
    for send in sends:
        send.wait()


def correlate(current, prior, tile_shift):
    hbm = pl.BlockSpec(memory_space=pltpu.HBM)
    return pl.pallas_call(
        correlate_kernel,
        out_shape=jax.ShapeDtypeStruct((OFFSETS, 16, 256), BF),
        in_specs=[pl.BlockSpec(memory_space=pltpu.SMEM), hbm, hbm],
        out_specs=hbm,
        scratch_shapes=[
            pltpu.VMEM((64, 16, 128), BF),
            pltpu.VMEM((64, 48, 128), BF),
            pltpu.VMEM((64, 16, 128), F32),
            pltpu.VMEM((72, 48, 128), F32),
            pltpu.VMEM((4, 24, 32, 128), BF),
            pltpu.VMEM((256, 256), F32),
            pltpu.VMEM((2, 4, SPAN, 3, 8, 256), F32),
            pltpu.VMEM(((BASE + 24) * SPAN * 8, 128), F32),
            pltpu.VMEM((2, OFFSETS, 16, 128), BF),
            pltpu.SemaphoreType.DMA((2, 4)),
            pltpu.SemaphoreType.DMA((2,)),
        ],
        compiler_params=pltpu.CompilerParams(vmem_limit_bytes=LIMIT),
        name="correlate",
    )(tile_shift, current, prior)


def local(sections, tile_shift, w_first, w_second, w_third, w_fourth, w_fifth):
    weights = (w_first.reshape(2, 2, 32), w_second, w_third, w_fourth, w_fifth.T)
    current, prior = share(sections, weights)
    current = current.reshape(64, 16, 128)
    prior = prior.reshape(64, 48, 128)
    shift = jnp.transpose(tile_shift, (0, 1, 3, 2)).reshape(2, 4)
    found = correlate(current, prior, shift)
    return jnp.transpose(found[None], (0, 2, 1, 3))


def solution(mesh):
    placed = (P("sec", None, "tile"), P("sec", "tile", None, None), P(), P(), P(), P(), P())
    return jax.shard_map(
        local, mesh=mesh, in_specs=placed, out_specs=P("sec", "tile", None, None), check_vma=False
    )
```

```python
import functools
import math

import jax
import jax.numpy as jnp
from jax import lax
from jax.experimental import pallas as pl
from jax.experimental.pallas import tpu as pltpu
from jax.sharding import PartitionSpec as P

REACH = 8
SPAN = 2 * REACH + 1
OFFSETS = SPAN * SPAN
BF = jnp.bfloat16
F32 = jnp.float32

ROWS = 256
CHUNK = 64
LIMIT = 60 * 2**20
SENT = (6, 12, 17)
GROUP = 8
HELD = 1
BASE = 7


def iota(shape, dim):
    return lax.broadcasted_iota(jnp.int32, shape, dim)


def dot(a, b):
    return jnp.dot(a, b, preferred_element_type=F32)


def expand_weights(w1, w2, w3, w4, w5, e1, e2, e3, e4, e5):
    pixel = iota((128, 128), 0)
    column = iota((128, 128), 1) // 32
    for k1 in range(2):
        wide = [
            jnp.broadcast_to(jnp.concatenate([w1[k1, kx : kx + 1].astype(F32)] * 4, axis=1), (128, 128))
            for kx in range(2)
        ]
        for g in range(16):
            phase = pixel - 2 * (4 * g + column)
            block = jnp.where(phase == 0, wide[0], jnp.where(phase == 1, wide[1], 0.0))
            e1[k1 * 128 : k1 * 128 + 128, g * 128 : g * 128 + 128] = block.astype(BF)

    def spread(pieces, rows, outs, count):
        bands = []
        for line in pieces:
            bands.append(
                jnp.concatenate(
                    [jnp.zeros((rows, outs), F32) if p is None else p for p in line], axis=1
                )
            )
        return jnp.concatenate(bands, axis=0).astype(BF)

    for k in range(2):
        pieces = [
            [w2[k, ci % 2].astype(F32) if ci // 2 == co else None for co in range(4)]
            for ci in range(8)
        ]
        e2[256 * k : 256 * k + 256] = spread(pieces, 32, 64, 4)
        pieces = [
            [w3[k, ci % 2].astype(F32) if ci // 2 == co else None for co in range(2)]
            for ci in range(4)
        ]
        e3[256 * k : 256 * k + 256] = spread(pieces, 64, 64, 2)
    e4[...] = spread(
        [[w4[...].astype(F32) if ci == co else None for co in range(4)] for ci in range(4)], 64, 64, 4
    )
    e5[...] = spread(
        [[jnp.transpose(w5[...].astype(F32)) if ci == co else None for co in range(4)] for ci in range(4)], 64, 32, 4
    )


def relu(x):
    return jnp.maximum(x, 0.0).astype(BF)


def encode_chunk(px, xs, a1, a2, a3, e1, e2, e3, e4, e5, perm):
    for part in range(CHUNK // 32):
        sorted_rows = dot(perm[...], px[part * 256 : part * 256 + 256, :]).astype(BF)
        for k in range(8):
            xs[k // 2, part * 32 : part * 32 + 32, (k % 2) * 128 : (k % 2) * 128 + 128] = sorted_rows[
                k * 32 : k * 32 + 32
            ]
    lhs = xs[...].reshape(4 * CHUNK, 256)
    for j in range(4):
        out = relu(dot(lhs, e1[:, 512 * j : 512 * j + 512]))
        out = out.reshape(2, 2, CHUNK, 512)
        for half in range(2):
            for k2 in range(2):
                a1[2 * j + half, :, 256 * k2 : 256 * k2 + 256] = out[
                    :, k2, :, 256 * half : 256 * half + 256
                ].reshape(2 * CHUNK, 256)
    for j in range(2):
        out = relu(dot(a1[4 * j : 4 * j + 4].reshape(8 * CHUNK, 512), e2[...]))
        out = out.reshape(4, 2, CHUNK, 256)
        for k3 in range(2):
            a2[4 * j : 4 * j + 4, :, 256 * k3 : 256 * k3 + 256] = out[:, k3]
    out = relu(dot(a2[...].reshape(8 * CHUNK, 512), e3[...])).reshape(4, 2, CHUNK, 128)
    a3[:, :, 0:128] = out[:, 0]
    a3[:, :, 128:256] = out[:, 1]
    out = relu(dot(a3[...].reshape(4 * CHUNK, 256), e4[...]))
    return dot(out, e5[...]).astype(BF).reshape(4, CHUNK, 128)


def share_kernel(
    px_hbm, w1_hbm, w2_hbm, w3_hbm, w4_hbm, w5_hbm, cur, prior,
    px, w1, w2, w3, w4, w5, bands, xs, a1, a2, a3, e1, e2, e3, e4, e5, perm,
    load_sem, px_sem, send_sem, cur_sem, prior_sem, halo_send, halo_recv, home_sem,
):
    s = lax.axis_index("sec")
    t = lax.axis_index("tile")
    secs = lax.axis_size("sec")
    tiles = lax.axis_size("tile")
    group = lax.rem(t, 4)
    member = lax.div(t, 4)
    chunks = ROWS // CHUNK
    pixels = 8 * CHUNK

    def chunk_at(phase):
        flip = jnp.int32(chunks - 1) - phase
        high = lax.rem(lax.div(member, 2) + lax.div(flip, 2), 2)
        return 2 * high + lax.rem(member + flip, 2)


    barrier = pltpu.get_barrier_semaphore()

    def greet(to_s, to_t):
        pl.semaphore_signal(
            barrier, inc=1, device_id=(to_s, to_t), device_id_type=pl.DeviceIdType.MESH
        )

    @pl.loop(1, tiles)
    def _(k):
        greet(s, lax.rem(t + k, tiles))

    @pl.when(s > 0)
    def _():
        @pl.loop(0, tiles)
        def _(k):
            greet(s - 1, lax.rem(t + k, tiles))

    loads = [
        pltpu.make_async_copy(a, b, load_sem.at[i])
        for i, (a, b) in enumerate(
            [(w1_hbm, w1), (w2_hbm, w2), (w3_hbm, w3), (w4_hbm, w4), (w5_hbm, w5)]
        )
    ]
    for load in loads:
        load.start()

    def fetch(phase):
        chunk = chunk_at(phase)
        return pltpu.make_async_copy(
            px_hbm.at[0, pl.ds(pl.multiple_of(chunk * pixels, pixels), pixels)],
            px.at[phase],
            px_sem.at[phase],
        )

    for phase in range(chunks):
        fetch(phase).start()

    r = iota((256, 256), 0)
    c = iota((256, 256), 1)
    perm[...] = jnp.where(8 * (r % 32) + r // 32 == c, 1.0, 0.0).astype(BF)
    for load in loads:
        load.wait()
    expand_weights(w1, w2, w3, w4, w5, e1, e2, e3, e4, e5)

    def band_of(to_t):
        return bands.at[:, pl.ds(pl.multiple_of(16 * to_t, 16), 16)]

    home = pltpu.make_async_copy(band_of(t), cur.at[member, group], home_sem)

    def encode_phase(phase):
        chunk = chunk_at(phase)
        fetch(phase).wait()
        done = encode_chunk(px.at[phase], xs, a1, a2, a3, e1, e2, e3, e4, e5, perm)
        bands[:, pl.ds(pl.multiple_of(chunk * CHUNK, CHUNK), CHUNK), :] = done

    def send_phase(phase):
        chunk = chunk_at(phase)

        def push(to_t, to_s, by, dst, sem):
            pltpu.make_async_remote_copy(
                src_ref=band_of(to_t),
                dst_ref=dst,
                send_sem=send_sem.at[by],
                recv_sem=sem,
                device_id=to_s,
                device_id_type=pl.DeviceIdType.MESH,
            ).start()

        @pl.when(s < secs - 1)
        def _():
            @pl.loop(0, CHUNK // 16)
            def _(k):
                to_t = chunk * (CHUNK // 16) + lax.rem(k + member, CHUNK // 16)
                push(to_t, (s + 1, to_t), 0, prior.at[member, group, :, 16:32], prior_sem.at[member])

                @pl.when(to_t == tiles // 2 - 1)
                def _():
                    push(to_t, (s + 1, to_t + 1), 2, prior.at[member, group, :, 0:16], halo_recv.at[0, member])

                @pl.when(to_t == tiles // 2)
                def _():
                    push(to_t, (s + 1, to_t - 1), 2, prior.at[member, group, :, 32:48], halo_recv.at[1, member])

        @pl.loop(0, CHUNK // 16)
        def _(k):
            to_t = chunk * (CHUNK // 16) + lax.rem(k + member, CHUNK // 16)

            @pl.when(to_t != t)
            def _():
                push(to_t, (s, to_t), 1, cur.at[member, group], cur_sem.at[0])

            @pl.when(to_t == t)
            def _():
                home.start()

    @pl.loop(0, chunks)
    def _(phase):
        encode_phase(phase)

        @pl.when(phase == HELD - 1)
        def _():
            @pl.when(s < secs - 1)
            def _():
                pl.semaphore_wait(barrier, 2 * tiles - 1)

            @pl.when(s == secs - 1)
            def _():
                pl.semaphore_wait(barrier, tiles - 1)

            @pl.loop(0, HELD)
            def _(before):
                send_phase(before)

        @pl.when(phase >= HELD)
        def _():
            send_phase(phase)

    def halo(to_t, row, side, g):
        return pltpu.make_async_remote_copy(
            src_ref=prior.at[g, :, :, 16:32],
            dst_ref=prior.at[g, :, :, row : row + 16],
            send_sem=halo_send.at[side, g],
            recv_sem=halo_recv.at[side, g],
            device_id=(s, to_t),
            device_id_type=pl.DeviceIdType.MESH,
        )

    has_next = t < tiles - 1
    has_last = t > 0

    def arrive(ref, sem):
        pltpu.make_async_copy(ref, ref, sem).wait()

    @pl.when(s > 0)
    def _():
        @pl.loop(0, 4)
        def _(k):
            g = chunk_at(k)
            arrive(prior.at[g, :, :, 16:32], prior_sem.at[g])

            @pl.when(has_next & (t != tiles // 2 - 1))
            def _():
                halo(t + 1, 0, 0, g).start()

            @pl.when(has_last & (t != tiles // 2))
            def _():
                halo(t - 1, 32, 1, g).start()

    home.wait()
    arrive(bands.at[:, 0:240], cur_sem.at[0])
    arrive(bands.at[:, 0:240], send_sem.at[1])

    @pl.when(s < secs - 1)
    def _():
        arrive(bands, send_sem.at[0])
        arrive(bands.at[:, 0:32], send_sem.at[2])

    @pl.when(s > 0)
    def _():
        @pl.loop(0, 4)
        def _(g):
            @pl.when(has_next & (t != tiles // 2 - 1))
            def _():
                halo(t + 1, 0, 0, g).wait_send()

            @pl.when(has_last & (t != tiles // 2))
            def _():
                halo(t - 1, 32, 1, g).wait_send()

            @pl.when(has_next)
            def _():
                arrive(prior.at[g, :, :, 32:48], halo_recv.at[1, g])

            @pl.when(has_last)
            def _():
                arrive(prior.at[g, :, :, 0:16], halo_recv.at[0, g])


def share(sections, weights):
    hbm = pl.BlockSpec(memory_space=pltpu.HBM)
    return pl.pallas_call(
        share_kernel,
        out_shape=(
            jax.ShapeDtypeStruct((4, 4, 4, 16, 128), BF),
            jax.ShapeDtypeStruct((4, 4, 4, 48, 128), BF),
        ),
        in_specs=[hbm] * 6,
        out_specs=(hbm, hbm),
        scratch_shapes=[
            pltpu.VMEM((ROWS // CHUNK, 8 * CHUNK, 128), BF),
            *[pltpu.VMEM(w.shape, BF) for w in weights],
            pltpu.VMEM((4, ROWS, 128), BF),
            pltpu.VMEM((4, CHUNK, 256), BF),
            pltpu.VMEM((8, 2 * CHUNK, 512), BF),
            pltpu.VMEM((8, CHUNK, 512), BF),
            pltpu.VMEM((4, CHUNK, 256), BF),
            pltpu.VMEM((256, 2048), BF),
            pltpu.VMEM((512, 256), BF),
            pltpu.VMEM((512, 128), BF),
            pltpu.VMEM((256, 256), BF),
            pltpu.VMEM((256, 128), BF),
            pltpu.VMEM((256, 256), BF),
            pltpu.SemaphoreType.DMA((5,)),
            pltpu.SemaphoreType.DMA((ROWS // CHUNK,)),
            pltpu.SemaphoreType.DMA((3,)),
            pltpu.SemaphoreType.DMA((1,)),
            pltpu.SemaphoreType.DMA((4,)),
            pltpu.SemaphoreType.DMA((2, 4)),
            pltpu.SemaphoreType.DMA((2, 4)),
            pltpu.SemaphoreType.DMA,
        ],
        compiler_params=pltpu.CompilerParams(
            vmem_limit_bytes=LIMIT, collective_id=0, has_side_effects=True
        ),
        name="share",
    )(sections, *weights)


def weave(main, *others):
    extra = [step for other in others for step in other]
    used = 0
    for n, step in enumerate(main):
        step()
        goal = len(extra) * (n + 1) // len(main)
        while used < goal:
            extra[used]()
            used += 1


def correlate_kernel(
    shift, cur_hbm, prior_hbm, out_hbm, cur, prior, cur32, wide, lhs, rhs, picked, rows, out, in_sem, out_sem
):
    s = lax.axis_index("sec")
    t = lax.axis_index("tile")
    loads = []
    for i in range(4):
        near = pl.ds(16 * i, 16)
        loads.append(
            (
                pltpu.make_async_copy(prior_hbm.at[near], prior.at[near], in_sem.at[0, i]),
                pltpu.make_async_copy(cur_hbm.at[near], cur.at[near], in_sem.at[1, i]),
            )
        )
    for pair in loads:
        for load in pair:
            load.start()
    wide[0:4] = jnp.zeros((4, 48, 128), F32)
    wide[68:72] = jnp.zeros((4, 48, 128), F32)

    row = iota((1, 48, 128), 1)
    first = jnp.where(t == 0, 16, 0)
    last = jnp.where(t == lax.axis_size("tile") - 1, 32, 48)
    last = jnp.where(s == 0, 0, last)
    inside = (row >= first) & (row < last)

    lane = iota((8, 128), 1)
    slot = lane // 32
    sub = iota((8, 128), 0)
    lane256 = iota((8, 256), 1)
    block = (lane256 % 32) // 8
    wide_lane = iota((32, 128), 1)

    def widen(member):
        def step(i):
            if i == 0:
                for load in loads[member]:
                    load.wait()
            q = 16 * member + 4 * i
            wide[4 + q : 8 + q] = jnp.where(inside, prior[q : q + 4].astype(F32), 0.0)
            cur32[q : q + 4] = cur[q : q + 4].astype(F32)

        return [functools.partial(step, i) for i in range(4)]

    def windows(tile):
        dy = shift[0, tile]

        def step(q):
            here = wide[16 * tile + q, pl.ds(8 + dy, 32), :]
            beside = wide[16 * tile + q + 1, pl.ds(8 + dy, 32), :]
            lhs[tile][0, q] = here.astype(BF)
            for e in range(1, 4):
                mixed = jnp.where(wide_lane < 32 * e, beside, here)
                lhs[tile][e, q] = pltpu.roll(mixed, 128 - 32 * e, 1).astype(BF)

        return [functools.partial(step, q) for q in range(23)]

    def masked(side, j):
        def step(u):
            y = (u % 4 - j) % 4 + 4 * (u // 4)
            for pair in range(2):
                left, right = [], []
                for m in (2 * pair, 2 * pair + 1):
                    q = 32 * side + 8 * j + 2 * m
                    a = jnp.broadcast_to(cur32[q, y : y + 1, :], (8, 128))
                    b = jnp.broadcast_to(cur32[q + 1, y : y + 1, :], (8, 128))
                    left.append(jnp.where(slot == sub, a, 0.0))
                    right.append(jnp.where(slot + 4 == sub, b, 0.0))
                at = u * 32 + 16 * pair
                rhs[j % 2][at : at + 16, 0:128] = jnp.concatenate(left, axis=0).astype(BF)
                rhs[j % 2][at : at + 16, 128:256] = jnp.concatenate(right, axis=0).astype(BF)

        return [functools.partial(step, u) for u in range(16)]

    def products(side, j):
        tile = 2 * side + j // 2
        dx = shift[1, tile]

        def step(group):
            places, parts = [], []
            for jj in group:
                place = 8 + dx + 32 * (j % 2) + jj
                e = lax.rem(place, 4)
                q = lax.div(place, 4)
                for m in range(6 if jj == 0 else 5):
                    places.append(jj + 8 * m)
                    parts.append(
                        jnp.concatenate([lhs[tile][e, q + 2 * m], lhs[tile][e, q + 2 * m + 1]], axis=1)
                    )
            product = lax.dot_general(
                jnp.concatenate(parts, axis=0),
                rhs[j % 2][...],
                (((1,), (1,)), ((), ())),
                preferred_element_type=F32,
            ).reshape(len(parts), 4, 8, 512)
            for jj in group:
                for ox in range(jj, SPAN, 8):
                    at = [places.index(ox + 8 * b) for b in range(4)]
                    for half in range(2):
                        lanes = slice(256 * half, 256 * half + 256)
                        for i in range(3):
                            piece = product[at[3], i + half, :, lanes]
                            for b in (2, 1, 0):
                                piece = jnp.where(block == b, product[at[b], i + half, :, lanes], piece)
                            picked[2 * side + half][j, ox, i] = piece

        return [functools.partial(step, range(g, g + GROUP)) for g in range(0, 8, GROUP)]

    def merge(side, half):
        source = picked[2 * side + half]

        def step(ox):
            for v in range(2):
                for i in range(3):
                    blocks = [source[j, ox, i, :, 128 * v : 128 * v + 128] for j in range(4)]
                    for k in range(4):
                        merged = blocks[(3 - k) % 4]
                        for u in (2, 1, 0):
                            merged = jnp.where(slot == u, blocks[(u - k) % 4], merged)
                        if k:
                            merged = pltpu.roll(merged, 128 - 32 * k, 1)
                        y = 4 * v + k
                        start = ((BASE + 8 * i - y) * SPAN + ox) * 8 + y
                        rows[half][pl.ds(start, 8, stride=8 * SPAN), :] = merged

        return [functools.partial(step, ox) for ox in range(SPAN)]

    sends = []

    def finish(side, half):
        def step(oy):
            start = (BASE + oy) * SPAN * 8
            done = rows[half][start : start + SPAN * 8, :] * (1.0 / math.sqrt(32))
            done = done.astype(BF).reshape(SPAN, 8, 128)
            out[side, oy * SPAN : oy * SPAN + SPAN, 8 * half : 8 * half + 8, :] = done
            if half == 1 and (oy + 1) in SENT:
                part = SENT.index(oy + 1)
                begin = SENT[part - 1] * SPAN if part else 0
                span = pl.ds(begin, (oy + 1) * SPAN - begin)
                send = pltpu.make_async_copy(
                    out.at[side, span],
                    out_hbm.at[span, :, pl.ds(128 * side, 128)],
                    out_sem.at[side, part],
                )
                send.start()
                sends.append(send)

        return [functools.partial(step, oy) for oy in range(SPAN)]

    def run(steps):
        for step in steps:
            step()

    def stage(side, extra, following):
        for j in range(4):
            after = masked(side, j + 1) if j < 3 else following
            weave(products(side, j), after, extra[j])

    def quarters(steps):
        return [steps[len(steps) * n // 4 : len(steps) * (n + 1) // 4] for n in range(4)]

    run(widen(0))
    run(widen(1))
    run(masked(0, 0))
    run(windows(0))
    stage(
        0, [widen(2) + windows(1)[:11], windows(1)[11:] + widen(3), windows(2), windows(3)], masked(1, 0),
    )
    stage(1, quarters(merge(0, 0) + finish(0, 0) + merge(0, 1) + finish(0, 1)), [])
    for half in range(2):
        run(merge(1, half))
        run(finish(1, half))
    for send in sends:
        send.wait()


def correlate(current, prior, tile_shift):
    hbm = pl.BlockSpec(memory_space=pltpu.HBM)
    return pl.pallas_call(
        correlate_kernel,
        out_shape=jax.ShapeDtypeStruct((OFFSETS, 16, 256), BF),
        in_specs=[pl.BlockSpec(memory_space=pltpu.SMEM), hbm, hbm],
        out_specs=hbm,
        scratch_shapes=[
            pltpu.VMEM((64, 16, 128), BF),
            pltpu.VMEM((64, 48, 128), BF),
            pltpu.VMEM((64, 16, 128), F32),
            pltpu.VMEM((72, 48, 128), F32),
            [pltpu.VMEM((4, 24, 32, 128), BF)] * 4,
            [pltpu.VMEM((512, 256), BF)] * 2,
            [pltpu.VMEM((4, SPAN, 3, 8, 256), F32)] * 4,
            [pltpu.VMEM(((BASE + 24) * SPAN * 8, 128), F32)] * 2,
            pltpu.VMEM((2, OFFSETS, 16, 128), BF),
            pltpu.SemaphoreType.DMA((2, 4)),
            pltpu.SemaphoreType.DMA((2, len(SENT))),
        ],
        compiler_params=pltpu.CompilerParams(vmem_limit_bytes=LIMIT),
        name="correlate",
    )(tile_shift, current, prior)


def local(sections, tile_shift, w_first, w_second, w_third, w_fourth, w_fifth):
    weights = (w_first.reshape(2, 2, 32), w_second, w_third, w_fourth, w_fifth.T)
    current, prior = share(sections, weights)
    current = current.reshape(64, 16, 128)
    prior = prior.reshape(64, 48, 128)
    shift = jnp.transpose(tile_shift, (0, 1, 3, 2)).reshape(2, 4)
    found = correlate(current, prior, shift)
    return jnp.transpose(found[None], (0, 2, 1, 3))


def solution(mesh):
    placed = (P("sec", None, "tile"), P("sec", "tile", None, None), P(), P(), P(), P(), P())
    return jax.shard_map(
        local, mesh=mesh, in_specs=placed, out_specs=P("sec", "tile", None, None), check_vma=False
    )
```

```python
import functools
import math

import jax
import jax.numpy as jnp
from jax import lax
from jax.experimental import pallas as pl
from jax.experimental.pallas import tpu as pltpu
from jax.sharding import PartitionSpec as P

REACH = 8
SPAN = 2 * REACH + 1
OFFSETS = SPAN * SPAN
BF = jnp.bfloat16
F32 = jnp.float32

ROWS = 256
CHUNK = 64
LIMIT = 60 * 2**20
SENT = (6, 12, 17)
GROUP = 8
HELD = 1
LINE = 8 * SPAN + 1
BASE = 7


def iota(shape, dim):
    return lax.broadcasted_iota(jnp.int32, shape, dim)


def dot(a, b):
    return jnp.dot(a, b, preferred_element_type=F32)


def expand_weights(w1, w2, w3, w4, w5, e1, e2, e3, e4, e5):
    pixel = iota((128, 128), 0)
    column = iota((128, 128), 1) // 32
    for k1 in range(2):
        wide = [
            jnp.broadcast_to(jnp.concatenate([w1[k1, kx : kx + 1].astype(F32)] * 4, axis=1), (128, 128))
            for kx in range(2)
        ]
        for g in range(16):
            phase = pixel - 2 * (4 * g + column)
            block = jnp.where(phase == 0, wide[0], jnp.where(phase == 1, wide[1], 0.0))
            e1[k1 * 128 : k1 * 128 + 128, g * 128 : g * 128 + 128] = block.astype(BF)

    def spread(pieces, rows, outs, count):
        bands = []
        for line in pieces:
            bands.append(
                jnp.concatenate(
                    [jnp.zeros((rows, outs), F32) if p is None else p for p in line], axis=1
                )
            )
        return jnp.concatenate(bands, axis=0).astype(BF)

    for k in range(2):
        pieces = [
            [w2[k, ci % 2].astype(F32) if ci // 2 == co else None for co in range(4)]
            for ci in range(8)
        ]
        e2[256 * k : 256 * k + 256] = spread(pieces, 32, 64, 4)
        pieces = [
            [w3[k, ci % 2].astype(F32) if ci // 2 == co else None for co in range(2)]
            for ci in range(4)
        ]
        e3[256 * k : 256 * k + 256] = spread(pieces, 64, 64, 2)
    e4[...] = spread(
        [[w4[...].astype(F32) if ci == co else None for co in range(4)] for ci in range(4)], 64, 64, 4
    )
    e5[...] = spread(
        [[jnp.transpose(w5[...].astype(F32)) if ci == co else None for co in range(4)] for ci in range(4)], 64, 32, 4
    )


def relu(x):
    return jnp.maximum(x, 0.0).astype(BF)


def encode_chunk(px, xs, a1, a2, a3, e1, e2, e3, e4, e5, perm):
    for part in range(CHUNK // 32):
        sorted_rows = dot(perm[...], px[part * 256 : part * 256 + 256, :]).astype(BF)
        for k in range(8):
            xs[k // 2, part * 32 : part * 32 + 32, (k % 2) * 128 : (k % 2) * 128 + 128] = sorted_rows[
                k * 32 : k * 32 + 32
            ]
    lhs = xs[...].reshape(4 * CHUNK, 256)
    for j in range(4):
        out = relu(dot(lhs, e1[:, 512 * j : 512 * j + 512]))
        out = out.reshape(2, 2, CHUNK, 512)
        for half in range(2):
            for k2 in range(2):
                a1[2 * j + half, :, 256 * k2 : 256 * k2 + 256] = out[
                    :, k2, :, 256 * half : 256 * half + 256
                ].reshape(2 * CHUNK, 256)
    for j in range(2):
        out = relu(dot(a1[4 * j : 4 * j + 4].reshape(8 * CHUNK, 512), e2[...]))
        out = out.reshape(4, 2, CHUNK, 256)
        for k3 in range(2):
            a2[4 * j : 4 * j + 4, :, 256 * k3 : 256 * k3 + 256] = out[:, k3]
    out = relu(dot(a2[...].reshape(8 * CHUNK, 512), e3[...])).reshape(4, 2, CHUNK, 128)
    a3[:, :, 0:128] = out[:, 0]
    a3[:, :, 128:256] = out[:, 1]
    out = relu(dot(a3[...].reshape(4 * CHUNK, 256), e4[...]))
    out = dot(out, e5[...]).astype(BF).reshape(4, CHUNK // 16, 16, 128)
    return jnp.stack([out[:, k] for k in range(CHUNK // 16)])


def share_kernel(
    px_hbm, w1_hbm, w2_hbm, w3_hbm, w4_hbm, w5_hbm, cur, prior,
    px, w1, w2, w3, w4, w5, bands, xs, a1, a2, a3, e1, e2, e3, e4, e5, perm,
    load_sem, px_sem, send_sem, cur_sem, prior_sem, halo_send, halo_recv, home_sem,
):
    s = lax.axis_index("sec")
    t = lax.axis_index("tile")
    secs = lax.axis_size("sec")
    tiles = lax.axis_size("tile")
    group = lax.rem(t, 4)
    member = lax.div(t, 4)
    chunks = ROWS // CHUNK
    pixels = 8 * CHUNK

    def chunk_at(phase):
        flip = jnp.int32(chunks - 1) - phase
        high = lax.rem(lax.div(member, 2) + lax.div(flip, 2), 2)
        return 2 * high + lax.rem(member + flip, 2)


    barrier = pltpu.get_barrier_semaphore()

    def greet(to_s, to_t):
        pl.semaphore_signal(
            barrier, inc=1, device_id=(to_s, to_t), device_id_type=pl.DeviceIdType.MESH
        )

    @pl.loop(1, tiles)
    def _(k):
        greet(s, lax.rem(t + k, tiles))

    @pl.when(s > 0)
    def _():
        @pl.loop(0, tiles)
        def _(k):
            greet(s - 1, lax.rem(t + k, tiles))

    loads = [
        pltpu.make_async_copy(a, b, load_sem.at[i])
        for i, (a, b) in enumerate(
            [(w1_hbm, w1), (w2_hbm, w2), (w3_hbm, w3), (w4_hbm, w4), (w5_hbm, w5)]
        )
    ]
    for load in loads:
        load.start()

    def fetch(phase):
        chunk = chunk_at(phase)
        return pltpu.make_async_copy(
            px_hbm.at[0, pl.ds(pl.multiple_of(chunk * pixels, pixels), pixels)],
            px.at[phase],
            px_sem.at[phase],
        )

    for phase in range(chunks):
        fetch(phase).start()

    r = iota((256, 256), 0)
    c = iota((256, 256), 1)
    perm[...] = jnp.where(8 * (r % 32) + r // 32 == c, 1.0, 0.0).astype(BF)
    for load in loads:
        load.wait()
    expand_weights(w1, w2, w3, w4, w5, e1, e2, e3, e4, e5)

    def band_of(to_t):
        return bands.at[to_t]

    home = pltpu.make_async_copy(band_of(t), cur.at[member, group], home_sem)

    def encode_phase(phase):
        chunk = chunk_at(phase)
        fetch(phase).wait()
        done = encode_chunk(px.at[phase], xs, a1, a2, a3, e1, e2, e3, e4, e5, perm)
        bands[pl.ds(chunk * (CHUNK // 16), CHUNK // 16)] = done

    def send_phase(phase):
        chunk = chunk_at(phase)

        def push(to_t, to_s, by, dst, sem):
            pltpu.make_async_remote_copy(
                src_ref=band_of(to_t),
                dst_ref=dst,
                send_sem=send_sem.at[by],
                recv_sem=sem,
                device_id=to_s,
                device_id_type=pl.DeviceIdType.MESH,
            ).start()

        @pl.when(s < secs - 1)
        def _():
            @pl.loop(0, CHUNK // 16)
            def _(k):
                to_t = chunk * (CHUNK // 16) + lax.rem(k + member, CHUNK // 16)
                push(to_t, (s + 1, to_t), 0, prior.at[1, member, group], prior_sem.at[member])

                @pl.when(to_t == tiles // 2 - 1)
                def _():
                    push(to_t, (s + 1, to_t + 1), 2, prior.at[0, member, group], halo_recv.at[0, member])

                @pl.when(to_t == tiles // 2)
                def _():
                    push(to_t, (s + 1, to_t - 1), 2, prior.at[2, member, group], halo_recv.at[1, member])

        @pl.loop(0, CHUNK // 16)
        def _(k):
            to_t = chunk * (CHUNK // 16) + lax.rem(k + member, CHUNK // 16)

            @pl.when(to_t != t)
            def _():
                push(to_t, (s, to_t), 1, cur.at[member, group], cur_sem.at[0])

            @pl.when(to_t == t)
            def _():
                home.start()

    @pl.loop(0, chunks)
    def _(phase):
        encode_phase(phase)

        @pl.when(phase == HELD - 1)
        def _():
            @pl.when(s < secs - 1)
            def _():
                pl.semaphore_wait(barrier, 2 * tiles - 1)

            @pl.when(s == secs - 1)
            def _():
                pl.semaphore_wait(barrier, tiles - 1)

            @pl.loop(0, HELD)
            def _(before):
                send_phase(before)

        @pl.when(phase >= HELD)
        def _():
            send_phase(phase)

    def halo(to_t, part, side, g):
        return pltpu.make_async_remote_copy(
            src_ref=prior.at[1, g],
            dst_ref=prior.at[part, g],
            send_sem=halo_send.at[side, g],
            recv_sem=halo_recv.at[side, g],
            device_id=(s, to_t),
            device_id_type=pl.DeviceIdType.MESH,
        )

    has_next = t < tiles - 1
    has_last = t > 0

    def arrive(ref, sem):
        pltpu.make_async_copy(ref, ref, sem).wait()

    @pl.when(s > 0)
    def _():
        @pl.loop(0, 4)
        def _(k):
            g = chunk_at(k)
            arrive(prior.at[1, g], prior_sem.at[g])

            @pl.when(has_next & (t != tiles // 2 - 1))
            def _():
                halo(t + 1, 0, 0, g).start()

            @pl.when(has_last & (t != tiles // 2))
            def _():
                halo(t - 1, 2, 1, g).start()

    home.wait()
    arrive(bands.at[0:15], cur_sem.at[0])
    arrive(bands.at[0:15], send_sem.at[1])

    @pl.when(s < secs - 1)
    def _():
        arrive(bands, send_sem.at[0])
        arrive(bands.at[0:2], send_sem.at[2])

    @pl.when(s > 0)
    def _():
        @pl.loop(0, 4)
        def _(g):
            @pl.when(has_next & (t != tiles // 2 - 1))
            def _():
                halo(t + 1, 0, 0, g).wait_send()

            @pl.when(has_last & (t != tiles // 2))
            def _():
                halo(t - 1, 2, 1, g).wait_send()

            @pl.when(has_next)
            def _():
                arrive(prior.at[2, g], halo_recv.at[1, g])

            @pl.when(has_last)
            def _():
                arrive(prior.at[0, g], halo_recv.at[0, g])


def share(sections, weights):
    hbm = pl.BlockSpec(memory_space=pltpu.HBM)
    return pl.pallas_call(
        share_kernel,
        out_shape=(
            jax.ShapeDtypeStruct((4, 4, 4, 16, 128), BF),
            jax.ShapeDtypeStruct((3, 4, 4, 4, 16, 128), BF),
        ),
        in_specs=[hbm] * 6,
        out_specs=(hbm, hbm),
        scratch_shapes=[
            pltpu.VMEM((ROWS // CHUNK, 8 * CHUNK, 128), BF),
            *[pltpu.VMEM(w.shape, BF) for w in weights],
            pltpu.VMEM((ROWS // 16, 4, 16, 128), BF),
            pltpu.VMEM((4, CHUNK, 256), BF),
            pltpu.VMEM((8, 2 * CHUNK, 512), BF),
            pltpu.VMEM((8, CHUNK, 512), BF),
            pltpu.VMEM((4, CHUNK, 256), BF),
            pltpu.VMEM((256, 2048), BF),
            pltpu.VMEM((512, 256), BF),
            pltpu.VMEM((512, 128), BF),
            pltpu.VMEM((256, 256), BF),
            pltpu.VMEM((256, 128), BF),
            pltpu.VMEM((256, 256), BF),
            pltpu.SemaphoreType.DMA((5,)),
            pltpu.SemaphoreType.DMA((ROWS // CHUNK,)),
            pltpu.SemaphoreType.DMA((3,)),
            pltpu.SemaphoreType.DMA((1,)),
            pltpu.SemaphoreType.DMA((4,)),
            pltpu.SemaphoreType.DMA((2, 4)),
            pltpu.SemaphoreType.DMA((2, 4)),
            pltpu.SemaphoreType.DMA,
        ],
        compiler_params=pltpu.CompilerParams(
            vmem_limit_bytes=LIMIT, collective_id=0, has_side_effects=True
        ),
        name="share",
    )(sections, *weights)


def weave(main, *others):
    extra = [step for other in others for step in other]
    used = 0
    for n, step in enumerate(main):
        step()
        goal = len(extra) * (n + 1) // len(main)
        while used < goal:
            extra[used]()
            used += 1


def correlate_kernel(
    shift, cur_hbm, prior_hbm, out_hbm, cur, prior, cur32, wide, both, above, below, rhs, picked, rows, out, in_sem, out_sem
):
    s = lax.axis_index("sec")
    t = lax.axis_index("tile")
    loads = []
    for i in range(4):
        near = pl.ds(16 * i, 16)
        loads.append(
            (
                pltpu.make_async_copy(prior_hbm.at[:, near], prior.at[:, near], in_sem.at[0, i]),
                pltpu.make_async_copy(cur_hbm.at[near], cur.at[near], in_sem.at[1, i]),
            )
        )
    for pair in loads:
        for load in pair:
            load.start()
    wide[0:4] = jnp.zeros((4, 48, 128), F32)
    wide[68:72] = jnp.zeros((4, 48, 128), F32)

    inside = [(s > 0) & (t > 0), s > 0, (s > 0) & (t < lax.axis_size("tile") - 1)]

    lane = iota((8, 128), 1)
    slot = lane // 32
    sub = iota((8, 128), 0)
    lane256 = iota((8, 256), 1)
    block = (lane256 % 32) // 8
    wide_lane = iota((32, 128), 1)

    def widen(member):
        def step(i):
            if i == 0:
                for load in loads[member]:
                    load.wait()
            q = 16 * member + 4 * i
            for part in range(3):
                values = prior[part, q : q + 4].astype(F32)
                wide[4 + q : 8 + q, 16 * part : 16 * part + 16] = jnp.where(inside[part], values, 0.0)
            cur32[q : q + 4] = cur[q : q + 4].astype(F32)

        return [functools.partial(step, i) for i in range(4)]

    def windows(tile):
        dy = shift[0, tile]
        kept = {}

        def step(q):
            here = wide[16 * tile + q, pl.ds(8 + dy, 32), :]
            beside = wide[16 * tile + q + 1, pl.ds(8 + dy, 32), :]
            kept[q] = [here]
            for e in range(1, 4):
                mixed = jnp.where(wide_lane < 32 * e, beside, here)
                kept[q].append(pltpu.roll(mixed, 128 - 32 * e, 1))
            for e in range(4):
                both[tile][e, q] = kept[q][e][8:24].astype(BF)
            for first in [q - 2] + ([q - 1, q] if q == 22 else []):
                if first >= 0:
                    second = min(first + 2, 22)
                    for e in range(4):
                        for rows_of, at in ((above, 0), (below, 24)):
                            pair = [kept[first][e][at : at + 8], kept[second][e][at : at + 8]]
                            rows_of[tile][e, first] = jnp.concatenate(pair, axis=0).astype(BF)

        return [functools.partial(step, q) for q in range(23)]

    def masked(side, j):
        def step(u):
            y = (u % 4 - j) % 4 + 4 * (u // 4)
            for pair in range(2):
                left, right = [], []
                for m in (2 * pair, 2 * pair + 1):
                    q = 32 * side + 8 * j + 2 * m
                    a = jnp.broadcast_to(cur32[q, y : y + 1, :], (8, 128))
                    b = jnp.broadcast_to(cur32[q + 1, y : y + 1, :], (8, 128))
                    left.append(jnp.where(slot == sub, a, 0.0))
                    right.append(jnp.where(slot + 4 == sub, b, 0.0))
                at = u * 32 + 16 * pair
                rhs[j % 2][at : at + 16, 0:128] = jnp.concatenate(left, axis=0).astype(BF)
                rhs[j % 2][at : at + 16, 128:256] = jnp.concatenate(right, axis=0).astype(BF)

        return [functools.partial(step, u) for u in range(16)]

    def products(side, j):
        tile = 2 * side + j // 2
        dx = shift[1, tile]

        def times(parts, weights):
            return lax.dot_general(
                jnp.concatenate(parts, axis=0),
                weights,
                (((1,), (1,)), ((), ())),
                preferred_element_type=F32,
            ).reshape(len(parts), 2, 8, weights.shape[0])

        def step(group):
            places, parts, pairs, tops, ends = [], [], [], [], []
            for jj in group:
                place = 8 + dx + 32 * (j % 2) + jj
                e = lax.rem(place, 4)
                q = lax.div(place, 4)

                def window(source, m):
                    return jnp.concatenate([source[tile][e, q + 2 * m], source[tile][e, q + 2 * m + 1]], axis=1)

                for m in range(6 if jj == 0 else 5):
                    places.append(jj + 8 * m)
                    parts.append(window(both, m))
                for m in range(0, 6, 2):
                    pairs += [jj + 8 * m, jj + 8 * m + 8]
                    tops.append(window(above, m))
                    ends.append(window(below, m))
            weights = rhs[j % 2]
            middle = times(parts, weights[...])
            top = times(tops, weights[0:256])
            end = times(ends, weights[256:512])

            def rows_at(place, half, i):
                if i + half == 0:
                    return top[pairs.index(place) // 2, pairs.index(place) % 2]
                if i + half == 3:
                    return end[pairs.index(place) // 2, pairs.index(place) % 2]
                return middle[places.index(place), i + half - 1, :, 256 * half : 256 * half + 256]

            for jj in group:
                for ox in range(jj, SPAN, 8):
                    for half in range(2):
                        for i in range(3):
                            piece = rows_at(ox + 24, half, i)
                            for b in (2, 1, 0):
                                piece = jnp.where(block == b, rows_at(ox + 8 * b, half, i), piece)
                            picked[2 * side + half][j, ox, i] = piece

        return [functools.partial(step, range(g, g + GROUP)) for g in range(0, 8, GROUP)]

    def merge(side, half):
        source = picked[2 * side + half]

        def step(ox):
            for v in range(2):
                for i in range(3):
                    blocks = [source[j, ox, i, :, 128 * v : 128 * v + 128] for j in range(4)]
                    for k in range(4):
                        merged = blocks[(3 - k) % 4]
                        for u in (2, 1, 0):
                            merged = jnp.where(slot == u, blocks[(u - k) % 4], merged)
                        if k:
                            merged = pltpu.roll(merged, 128 - 32 * k, 1)
                        y = 4 * v + k
                        start = (BASE + 8 * i - y) * LINE + ox * 8 + y
                        rows[half][pl.ds(start, 8, stride=LINE), :] = merged

        return [functools.partial(step, ox) for ox in range(SPAN)]

    sends = []

    def finish(side, half):
        def step(oy):
            start = (BASE + oy) * LINE
            done = rows[half][start : start + SPAN * 8, :] * (1.0 / math.sqrt(32))
            done = done.astype(BF).reshape(SPAN, 8, 128)
            out[side, oy * SPAN : oy * SPAN + SPAN, 8 * half : 8 * half + 8, :] = done
            if half == 1 and (oy + 1) in SENT:
                part = SENT.index(oy + 1)
                begin = SENT[part - 1] * SPAN if part else 0
                span = pl.ds(begin, (oy + 1) * SPAN - begin)
                send = pltpu.make_async_copy(
                    out.at[side, span],
                    out_hbm.at[span, :, pl.ds(128 * side, 128)],
                    out_sem.at[side, part],
                )
                send.start()
                sends.append(send)

        return [functools.partial(step, oy) for oy in range(SPAN)]

    def run(steps):
        for step in steps:
            step()

    def stage(side, extra, following):
        for j in range(4):
            after = masked(side, j + 1) if j < 3 else following
            weave(products(side, j), after, extra[j])

    def quarters(steps):
        return [steps[len(steps) * n // 4 : len(steps) * (n + 1) // 4] for n in range(4)]

    run(widen(0))
    run(widen(1))
    run(masked(0, 0))
    run(windows(0))
    beside = windows(1)
    stage(
        0, [widen(2) + beside[:11], beside[11:] + widen(3), windows(2), windows(3)], masked(1, 0),
    )
    stage(1, quarters(merge(0, 0) + finish(0, 0) + merge(0, 1) + finish(0, 1)), [])
    for half in range(2):
        run(merge(1, half))
        run(finish(1, half))
    for send in sends:
        send.wait()


def correlate(current, prior, tile_shift):
    hbm = pl.BlockSpec(memory_space=pltpu.HBM)
    return pl.pallas_call(
        correlate_kernel,
        out_shape=jax.ShapeDtypeStruct((OFFSETS, 16, 256), BF),
        in_specs=[pl.BlockSpec(memory_space=pltpu.SMEM), hbm, hbm],
        out_specs=hbm,
        scratch_shapes=[
            pltpu.VMEM((64, 16, 128), BF),
            pltpu.VMEM((3, 64, 16, 128), BF),
            pltpu.VMEM((64, 16, 128), F32),
            pltpu.VMEM((72, 48, 128), F32),
            [pltpu.VMEM((4, 24, 16, 128), BF)] * 4,
            [pltpu.VMEM((4, 24, 16, 128), BF)] * 4,
            [pltpu.VMEM((4, 24, 16, 128), BF)] * 4,
            [pltpu.VMEM((512, 256), BF)] * 2,
            [pltpu.VMEM((4, SPAN, 3, 8, 256), F32)] * 4,
            [pltpu.VMEM(((BASE + 24) * LINE, 128), F32)] * 2,
            pltpu.VMEM((2, OFFSETS, 16, 128), BF),
            pltpu.SemaphoreType.DMA((2, 4)),
            pltpu.SemaphoreType.DMA((2, len(SENT))),
        ],
        compiler_params=pltpu.CompilerParams(vmem_limit_bytes=LIMIT),
        name="correlate",
    )(tile_shift, current, prior)


def local(sections, tile_shift, w_first, w_second, w_third, w_fourth, w_fifth):
    weights = (w_first.reshape(2, 2, 32), w_second, w_third, w_fourth, w_fifth.T)
    current, prior = share(sections, weights)
    current = current.reshape(64, 16, 128)
    prior = prior.reshape(3, 64, 16, 128)
    shift = jnp.transpose(tile_shift, (0, 1, 3, 2)).reshape(2, 4)
    found = correlate(current, prior, shift)
    return jnp.transpose(found[None], (0, 2, 1, 3))


def solution(mesh):
    placed = (P("sec", None, "tile"), P("sec", "tile", None, None), P(), P(), P(), P(), P())
    return jax.shard_map(
        local, mesh=mesh, in_specs=placed, out_specs=P("sec", "tile", None, None), check_vma=False
    )
```

```python
import functools
import math

import jax
import jax.numpy as jnp
from jax import lax
from jax.experimental import pallas as pl
from jax.experimental.pallas import tpu as pltpu
from jax.sharding import PartitionSpec as P

REACH = 8
SPAN = 2 * REACH + 1
OFFSETS = SPAN * SPAN
BF = jnp.bfloat16
F32 = jnp.float32

ROWS = 256
CHUNK = 64
LIMIT = 60 * 2**20
SENT = (6, 12, 17)
GROUP = 8
HELD = 1
LINE = 8 * SPAN + 1
BASE = 7


def iota(shape, dim):
    return lax.broadcasted_iota(jnp.int32, shape, dim)


def dot(a, b):
    return jnp.dot(a, b, preferred_element_type=F32)


def expand_weights(w1, w2, w3, w4, w5, e1, e2, e3, e4, e5):
    pixel = iota((128, 128), 0)
    column = iota((128, 128), 1) // 32
    for k1 in range(2):
        wide = [
            jnp.broadcast_to(jnp.concatenate([w1[k1, kx : kx + 1].astype(F32)] * 4, axis=1), (128, 128))
            for kx in range(2)
        ]
        for g in range(16):
            phase = pixel - 2 * (4 * g + column)
            block = jnp.where(phase == 0, wide[0], jnp.where(phase == 1, wide[1], 0.0))
            e1[k1 * 128 : k1 * 128 + 128, g * 128 : g * 128 + 128] = block.astype(BF)

    def spread(pieces, rows, outs, count):
        bands = []
        for line in pieces:
            bands.append(
                jnp.concatenate(
                    [jnp.zeros((rows, outs), F32) if p is None else p for p in line], axis=1
                )
            )
        return jnp.concatenate(bands, axis=0).astype(BF)

    for k in range(2):
        pieces = [
            [w2[k, ci % 2].astype(F32) if ci // 2 == co else None for co in range(4)]
            for ci in range(8)
        ]
        e2[256 * k : 256 * k + 256] = spread(pieces, 32, 64, 4)
        pieces = [
            [w3[k, ci % 2].astype(F32) if ci // 2 == co else None for co in range(2)]
            for ci in range(4)
        ]
        e3[256 * k : 256 * k + 256] = spread(pieces, 64, 64, 2)
    e4[...] = spread(
        [[w4[...].astype(F32) if ci == co else None for co in range(4)] for ci in range(4)], 64, 64, 4
    )
    e5[...] = spread(
        [[jnp.transpose(w5[...].astype(F32)) if ci == co else None for co in range(4)] for ci in range(4)], 64, 32, 4
    )


def relu(x):
    return jnp.maximum(x, 0.0).astype(BF)


def encode_chunk(px, xs, a1, a2, a3, e1, e2, e3, e4, e5, perm):
    for part in range(CHUNK // 32):
        sorted_rows = dot(perm[...], px[part * 256 : part * 256 + 256, :]).astype(BF)
        for k in range(8):
            xs[k // 2, part * 32 : part * 32 + 32, (k % 2) * 128 : (k % 2) * 128 + 128] = sorted_rows[
                k * 32 : k * 32 + 32
            ]
    lhs = xs[...].reshape(4 * CHUNK, 256)
    for j in range(4):
        out = relu(dot(lhs, e1[:, 512 * j : 512 * j + 512]))
        out = out.reshape(2, 2, CHUNK, 512)
        for half in range(2):
            for k2 in range(2):
                a1[2 * j + half, :, 256 * k2 : 256 * k2 + 256] = out[
                    :, k2, :, 256 * half : 256 * half + 256
                ].reshape(2 * CHUNK, 256)
    for j in range(2):
        out = relu(dot(a1[4 * j : 4 * j + 4].reshape(8 * CHUNK, 512), e2[...]))
        out = out.reshape(4, 2, CHUNK, 256)
        for k3 in range(2):
            a2[4 * j : 4 * j + 4, :, 256 * k3 : 256 * k3 + 256] = out[:, k3]
    out = relu(dot(a2[...].reshape(8 * CHUNK, 512), e3[...])).reshape(4, 2, CHUNK, 128)
    a3[:, :, 0:128] = out[:, 0]
    a3[:, :, 128:256] = out[:, 1]
    out = relu(dot(a3[...].reshape(4 * CHUNK, 256), e4[...]))
    out = dot(out, e5[...]).astype(BF).reshape(4, CHUNK // 16, 16, 128)
    return jnp.stack([out[:, k] for k in range(CHUNK // 16)])


def share_kernel(
    px_hbm, w1_hbm, w2_hbm, w3_hbm, w4_hbm, w5_hbm, cur, prior,
    px, w1, w2, w3, w4, w5, bands, xs, a1, a2, a3, e1, e2, e3, e4, e5, perm,
    load_sem, px_sem, send_sem, cur_sem, prior_sem, halo_send, halo_recv, home_sem,
):
    s = lax.axis_index("sec")
    t = lax.axis_index("tile")
    secs = lax.axis_size("sec")
    tiles = lax.axis_size("tile")
    group = lax.rem(t, 4)
    member = lax.div(t, 4)
    chunks = ROWS // CHUNK
    pixels = 8 * CHUNK

    def chunk_at(phase):
        flip = jnp.int32(chunks - 1) - phase
        high = lax.rem(lax.div(member, 2) + lax.div(flip, 2), 2)
        return 2 * high + lax.rem(member + flip, 2)


    barrier = pltpu.get_barrier_semaphore()

    def greet(to_s, to_t):
        pl.semaphore_signal(
            barrier, inc=1, device_id=(to_s, to_t), device_id_type=pl.DeviceIdType.MESH
        )

    @pl.loop(1, tiles)
    def _(k):
        greet(s, lax.rem(t + k, tiles))

    @pl.when(s > 0)
    def _():
        @pl.loop(0, tiles)
        def _(k):
            greet(s - 1, lax.rem(t + k, tiles))

    loads = [
        pltpu.make_async_copy(a, b, load_sem.at[i])
        for i, (a, b) in enumerate(
            [(w1_hbm, w1), (w2_hbm, w2), (w3_hbm, w3), (w4_hbm, w4), (w5_hbm, w5)]
        )
    ]
    for load in loads:
        load.start()

    def fetch(phase):
        chunk = chunk_at(phase)
        return pltpu.make_async_copy(
            px_hbm.at[0, pl.ds(pl.multiple_of(chunk * pixels, pixels), pixels)],
            px.at[phase],
            px_sem.at[phase],
        )

    for phase in range(chunks):
        fetch(phase).start()

    r = iota((256, 256), 0)
    c = iota((256, 256), 1)
    perm[...] = jnp.where(8 * (r % 32) + r // 32 == c, 1.0, 0.0).astype(BF)
    for load in loads:
        load.wait()
    expand_weights(w1, w2, w3, w4, w5, e1, e2, e3, e4, e5)

    def band_of(to_t):
        return bands.at[to_t]

    home = pltpu.make_async_copy(band_of(t), cur.at[member, group], home_sem)

    def encode_phase(phase):
        chunk = chunk_at(phase)
        fetch(phase).wait()
        done = encode_chunk(px.at[phase], xs, a1, a2, a3, e1, e2, e3, e4, e5, perm)
        bands[pl.ds(chunk * (CHUNK // 16), CHUNK // 16)] = done

    def send_phase(phase):
        chunk = chunk_at(phase)

        def push(to_t, to_s, by, dst, sem):
            pltpu.make_async_remote_copy(
                src_ref=band_of(to_t),
                dst_ref=dst,
                send_sem=send_sem.at[by],
                recv_sem=sem,
                device_id=to_s,
                device_id_type=pl.DeviceIdType.MESH,
            ).start()

        @pl.when(s < secs - 1)
        def _():
            @pl.loop(0, CHUNK // 16)
            def _(k):
                to_t = chunk * (CHUNK // 16) + lax.rem(k + member, CHUNK // 16)
                push(to_t, (s + 1, to_t), 0, prior.at[1, member, group], prior_sem.at[member])

                @pl.when(to_t == tiles // 2 - 1)
                def _():
                    push(to_t, (s + 1, to_t + 1), 2, prior.at[0, member, group], halo_recv.at[0, member])

                @pl.when(to_t == tiles // 2)
                def _():
                    push(to_t, (s + 1, to_t - 1), 2, prior.at[2, member, group], halo_recv.at[1, member])

        @pl.loop(0, CHUNK // 16)
        def _(k):
            to_t = chunk * (CHUNK // 16) + lax.rem(k + member, CHUNK // 16)

            @pl.when(to_t != t)
            def _():
                push(to_t, (s, to_t), 1, cur.at[member, group], cur_sem.at[0])

            @pl.when(to_t == t)
            def _():
                home.start()

    @pl.loop(0, chunks)
    def _(phase):
        encode_phase(phase)

        @pl.when(phase == HELD - 1)
        def _():
            @pl.when(s < secs - 1)
            def _():
                pl.semaphore_wait(barrier, 2 * tiles - 1)

            @pl.when(s == secs - 1)
            def _():
                pl.semaphore_wait(barrier, tiles - 1)

            @pl.loop(0, HELD)
            def _(before):
                send_phase(before)

        @pl.when(phase >= HELD)
        def _():
            send_phase(phase)

    def halo(to_t, part, side, g):
        return pltpu.make_async_remote_copy(
            src_ref=prior.at[1, g],
            dst_ref=prior.at[part, g],
            send_sem=halo_send.at[side, g],
            recv_sem=halo_recv.at[side, g],
            device_id=(s, to_t),
            device_id_type=pl.DeviceIdType.MESH,
        )

    has_next = t < tiles - 1
    has_last = t > 0

    def arrive(ref, sem):
        pltpu.make_async_copy(ref, ref, sem).wait()

    @pl.when(s > 0)
    def _():
        @pl.loop(0, 4)
        def _(k):
            g = chunk_at(k)
            arrive(prior.at[1, g], prior_sem.at[g])

            @pl.when(has_next & (t != tiles // 2 - 1))
            def _():
                halo(t + 1, 0, 0, g).start()

            @pl.when(has_last & (t != tiles // 2))
            def _():
                halo(t - 1, 2, 1, g).start()

    home.wait()
    arrive(bands.at[0:15], cur_sem.at[0])
    arrive(bands.at[0:15], send_sem.at[1])

    @pl.when(s < secs - 1)
    def _():
        arrive(bands, send_sem.at[0])
        arrive(bands.at[0:2], send_sem.at[2])

    @pl.when(s > 0)
    def _():
        @pl.loop(0, 4)
        def _(g):
            @pl.when(has_next & (t != tiles // 2 - 1))
            def _():
                halo(t + 1, 0, 0, g).wait_send()

            @pl.when(has_last & (t != tiles // 2))
            def _():
                halo(t - 1, 2, 1, g).wait_send()

            @pl.when(has_next)
            def _():
                arrive(prior.at[2, g], halo_recv.at[1, g])

            @pl.when(has_last)
            def _():
                arrive(prior.at[0, g], halo_recv.at[0, g])


def share(sections, weights):
    hbm = pl.BlockSpec(memory_space=pltpu.HBM)
    return pl.pallas_call(
        share_kernel,
        out_shape=(
            jax.ShapeDtypeStruct((4, 4, 4, 16, 128), BF),
            jax.ShapeDtypeStruct((3, 4, 4, 4, 16, 128), BF),
        ),
        in_specs=[hbm] * 6,
        out_specs=(hbm, hbm),
        scratch_shapes=[
            pltpu.VMEM((ROWS // CHUNK, 8 * CHUNK, 128), BF),
            *[pltpu.VMEM(w.shape, BF) for w in weights],
            pltpu.VMEM((ROWS // 16, 4, 16, 128), BF),
            pltpu.VMEM((4, CHUNK, 256), BF),
            pltpu.VMEM((8, 2 * CHUNK, 512), BF),
            pltpu.VMEM((8, CHUNK, 512), BF),
            pltpu.VMEM((4, CHUNK, 256), BF),
            pltpu.VMEM((256, 2048), BF),
            pltpu.VMEM((512, 256), BF),
            pltpu.VMEM((512, 128), BF),
            pltpu.VMEM((256, 256), BF),
            pltpu.VMEM((256, 128), BF),
            pltpu.VMEM((256, 256), BF),
            pltpu.SemaphoreType.DMA((5,)),
            pltpu.SemaphoreType.DMA((ROWS // CHUNK,)),
            pltpu.SemaphoreType.DMA((3,)),
            pltpu.SemaphoreType.DMA((1,)),
            pltpu.SemaphoreType.DMA((4,)),
            pltpu.SemaphoreType.DMA((2, 4)),
            pltpu.SemaphoreType.DMA((2, 4)),
            pltpu.SemaphoreType.DMA,
        ],
        compiler_params=pltpu.CompilerParams(
            vmem_limit_bytes=LIMIT, collective_id=0, has_side_effects=True
        ),
        name="share",
    )(sections, *weights)


def weave(main, *others):
    extra = [step for other in others for step in other]
    used = 0
    for n, step in enumerate(main):
        step()
        goal = len(extra) * (n + 1) // len(main)
        while used < goal:
            extra[used]()
            used += 1


def correlate_kernel(
    shift, cur_hbm, prior_hbm, out_hbm, cur, prior, cur32, wide, both, above, below, rhs, picked, rows, out, in_sem, out_sem
):
    s = lax.axis_index("sec")
    t = lax.axis_index("tile")
    loads = []
    for i in range(4):
        near = pl.ds(16 * i, 16)
        loads.append(
            (
                pltpu.make_async_copy(prior_hbm.at[:, near], prior.at[:, near], in_sem.at[0, i]),
                pltpu.make_async_copy(cur_hbm.at[near], cur.at[near], in_sem.at[1, i]),
            )
        )
    for pair in loads:
        for load in pair:
            load.start()
    wide[0:4] = jnp.zeros((4, 48, 128), F32)
    wide[68:72] = jnp.zeros((4, 48, 128), F32)

    inside = [(s > 0) & (t > 0), s > 0, (s > 0) & (t < lax.axis_size("tile") - 1)]

    lane = iota((8, 128), 1)
    slot = lane // 32
    sub = iota((8, 128), 0)
    lane256 = iota((8, 256), 1)
    block = (lane256 % 32) // 8
    wide_lane = iota((32, 128), 1)

    def widen(member):
        def step(i):
            if i == 0:
                for load in loads[member]:
                    load.wait()
            q = 16 * member + 4 * i
            for part in range(3):
                values = prior[part, q : q + 4].astype(F32)
                wide[4 + q : 8 + q, 16 * part : 16 * part + 16] = jnp.where(inside[part], values, 0.0)
            cur32[q : q + 4] = cur[q : q + 4].astype(F32)

        return [functools.partial(step, i) for i in range(4)]

    def windows(tile):
        dy = shift[0, tile]
        kept = {}

        def step(q):
            here = wide[16 * tile + q, pl.ds(8 + dy, 32), :]
            beside = wide[16 * tile + q + 1, pl.ds(8 + dy, 32), :]
            kept[q] = [here]
            for e in range(1, 4):
                mixed = jnp.where(wide_lane < 32 * e, beside, here)
                kept[q].append(pltpu.roll(mixed, 128 - 32 * e, 1))
            for e in range(4):
                both[tile][e, q] = kept[q][e][8:24].astype(BF)
            for first in [q - 2] + ([q - 1, q] if q == 22 else []):
                if first >= 0:
                    second = min(first + 2, 22)
                    for e in range(4):
                        for rows_of, at in ((above, 0), (below, 24)):
                            pair = [kept[first][e][at : at + 8], kept[second][e][at : at + 8]]
                            rows_of[tile][e, first] = jnp.concatenate(pair, axis=0).astype(BF)

        return [functools.partial(step, q) for q in range(23)]

    def masked(side, j):
        def step(u):
            y = (u % 4 - j) % 4 + 4 * (u // 4)
            for pair in range(2):
                left, right = [], []
                for m in (2 * pair, 2 * pair + 1):
                    q = 32 * side + 8 * j + 2 * m
                    a = jnp.broadcast_to(cur32[q, y : y + 1, :], (8, 128))
                    b = jnp.broadcast_to(cur32[q + 1, y : y + 1, :], (8, 128))
                    left.append(jnp.where(slot == sub, a, 0.0))
                    right.append(jnp.where(slot + 4 == sub, b, 0.0))
                at = u * 32 + 16 * pair
                rhs[j % 2][at : at + 16, 0:128] = jnp.concatenate(left, axis=0).astype(BF)
                rhs[j % 2][at : at + 16, 128:256] = jnp.concatenate(right, axis=0).astype(BF)

        return [functools.partial(step, u) for u in range(16)]

    def products(side, j):
        tile = 2 * side + j // 2
        dx = shift[1, tile]

        def times(parts, weights):
            return lax.dot_general(
                jnp.concatenate(parts, axis=0),
                weights,
                (((1,), (1,)), ((), ())),
                preferred_element_type=F32,
            ).reshape(len(parts), 2, 8, weights.shape[0])

        def step(group):
            places, parts, pairs, tops, ends = [], [], [], [], []
            for jj in group:
                place = 8 + dx + 32 * (j % 2) + jj
                e = lax.rem(place, 4)
                q = lax.div(place, 4)

                def window(source, m):
                    return jnp.concatenate([source[tile][e, q + 2 * m], source[tile][e, q + 2 * m + 1]], axis=1)

                for m in range(6 if jj == 0 else 5):
                    places.append(jj + 8 * m)
                    parts.append(window(both, m))
                for m in range(0, 6, 2):
                    pairs += [jj + 8 * m, jj + 8 * m + 8]
                    tops.append(window(above, m))
                    ends.append(window(below, m))
            weights = rhs[j % 2]
            middle = times(parts, weights[...])
            top = times(tops, weights[0:256])
            end = times(ends, weights[256:512])

            def rows_at(place, half, i):
                if i + half == 0:
                    return top[pairs.index(place) // 2, pairs.index(place) % 2]
                if i + half == 3:
                    return end[pairs.index(place) // 2, pairs.index(place) % 2]
                return middle[places.index(place), i + half - 1, :, 256 * half : 256 * half + 256]

            for jj in group:
                for ox in range(jj, SPAN, 8):
                    for half in range(2):
                        for i in range(3):
                            piece = rows_at(ox + 24, half, i)
                            for b in (2, 1, 0):
                                piece = jnp.where(block == b, rows_at(ox + 8 * b, half, i), piece)
                            picked[2 * side + half][j, ox, i] = piece

        return [functools.partial(step, range(g, g + GROUP)) for g in range(0, 8, GROUP)]

    def merge(side, half):
        source = picked[2 * side + half]

        def step(ox):
            for v in range(2):
                for i in range(3):
                    blocks = [source[j, ox, i, :, 128 * v : 128 * v + 128] for j in range(4)]
                    for k in range(4):
                        merged = blocks[(3 - k) % 4]
                        for u in (2, 1, 0):
                            merged = jnp.where(slot == u, blocks[(u - k) % 4], merged)
                        if k:
                            merged = pltpu.roll(merged, 128 - 32 * k, 1)
                        y = 4 * v + k
                        start = (BASE + 8 * i - y) * LINE + ox * 8 + y
                        rows[half][pl.ds(start, 8, stride=LINE), :] = merged

        return [functools.partial(step, ox) for ox in range(SPAN)]

    sends = []

    def finish(side, half):
        def step(oy):
            start = (BASE + oy) * LINE
            done = rows[half][start : start + SPAN * 8, :] * (1.0 / math.sqrt(32))
            done = done.astype(BF).reshape(SPAN, 8, 128)
            out[side, oy * SPAN : oy * SPAN + SPAN, 8 * half : 8 * half + 8, :] = done
            if half == 1 and (oy + 1) in SENT:
                part = SENT.index(oy + 1)
                begin = SENT[part - 1] * SPAN if part else 0
                span = pl.ds(begin, (oy + 1) * SPAN - begin)
                send = pltpu.make_async_copy(
                    out.at[side, span],
                    out_hbm.at[span, :, pl.ds(128 * side, 128)],
                    out_sem.at[side, part],
                )
                send.start()
                sends.append(send)

        return [functools.partial(step, oy) for oy in range(SPAN)]

    def run(steps):
        for step in steps:
            step()

    def stage(side, extra, following):
        for j in range(4):
            after = masked(side, j + 1) if j < 3 else following
            weave(products(side, j), after, extra[j])

    def quarters(steps):
        return [steps[len(steps) * n // 4 : len(steps) * (n + 1) // 4] for n in range(4)]

    run(widen(0))
    run(widen(1))
    run(masked(0, 0))
    run(windows(0))
    beside = windows(1)
    stage(
        0, [widen(2) + beside[:11], beside[11:] + widen(3), windows(2), windows(3)], masked(1, 0),
    )
    stage(1, quarters(merge(0, 0) + finish(0, 0) + merge(0, 1) + finish(0, 1)), [])
    for half in range(2):
        run(merge(1, half))
        run(finish(1, half))
    for send in sends:
        send.wait()


def correlate(current, prior, tile_shift):
    hbm = pl.BlockSpec(memory_space=pltpu.HBM)
    return pl.pallas_call(
        correlate_kernel,
        out_shape=jax.ShapeDtypeStruct((OFFSETS, 16, 256), BF),
        in_specs=[pl.BlockSpec(memory_space=pltpu.SMEM), hbm, hbm],
        out_specs=hbm,
        scratch_shapes=[
            pltpu.VMEM((64, 16, 128), BF),
            pltpu.VMEM((3, 64, 16, 128), BF),
            pltpu.VMEM((64, 16, 128), F32),
            pltpu.VMEM((72, 48, 128), F32),
            [pltpu.VMEM((4, 24, 16, 128), BF)] * 4,
            [pltpu.VMEM((4, 24, 16, 128), BF)] * 4,
            [pltpu.VMEM((4, 24, 16, 128), BF)] * 4,
            [pltpu.VMEM((512, 256), BF)] * 2,
            [pltpu.VMEM((4, SPAN, 3, 8, 256), F32)] * 4,
            [pltpu.VMEM(((BASE + 25) * LINE, 128), F32)] * 2,
            pltpu.VMEM((2, OFFSETS, 16, 128), BF),
            pltpu.SemaphoreType.DMA((2, 4)),
            pltpu.SemaphoreType.DMA((2, len(SENT))),
        ],
        compiler_params=pltpu.CompilerParams(vmem_limit_bytes=LIMIT),
        name="correlate",
    )(tile_shift, current, prior)


def local(sections, tile_shift, w_first, w_second, w_third, w_fourth, w_fifth):
    weights = (w_first.reshape(2, 2, 32), w_second, w_third, w_fourth, w_fifth.T)
    current, prior = share(sections, weights)
    current = current.reshape(64, 16, 128)
    prior = prior.reshape(3, 64, 16, 128)
    shift = jnp.transpose(tile_shift, (0, 1, 3, 2)).reshape(2, 4)
    found = correlate(current, prior, shift)
    return jnp.transpose(found[None], (0, 2, 1, 3))


def solution(mesh):
    placed = (P("sec", None, "tile"), P("sec", "tile", None, None), P(), P(), P(), P(), P())
    return jax.shard_map(
        local, mesh=mesh, in_specs=placed, out_specs=P("sec", "tile", None, None), check_vma=False
    )
```

```python
import functools
import math

import jax
import jax.numpy as jnp
from jax import lax
from jax.experimental import pallas as pl
from jax.experimental.pallas import tpu as pltpu
from jax.sharding import PartitionSpec as P

REACH = 8
SPAN = 2 * REACH + 1
OFFSETS = SPAN * SPAN
BF = jnp.bfloat16
F32 = jnp.float32

ROWS = 256
CHUNK = 64
LIMIT = 60 * 2**20
SENT = (6, 12, 17)
GROUP = 8
HELD = 1
LINE = 8 * SPAN + 1
BASE = 7


def iota(shape, dim):
    return lax.broadcasted_iota(jnp.int32, shape, dim)


def dot(a, b):
    return jnp.dot(a, b, preferred_element_type=F32)


def expand_weights(w1, w2, w3, w4, w5, e1, e2, e3, e4, e5):
    pixel = iota((128, 128), 0)
    column = iota((128, 128), 1) // 32
    for k1 in range(2):
        wide = [
            jnp.broadcast_to(jnp.concatenate([w1[k1, kx : kx + 1].astype(F32)] * 4, axis=1), (128, 128))
            for kx in range(2)
        ]
        for g in range(16):
            phase = pixel - 2 * (4 * g + column)
            block = jnp.where(phase == 0, wide[0], jnp.where(phase == 1, wide[1], 0.0))
            e1[k1 * 128 : k1 * 128 + 128, g * 128 : g * 128 + 128] = block.astype(BF)

    def spread(pieces, rows, outs, count):
        bands = []
        for line in pieces:
            bands.append(
                jnp.concatenate(
                    [jnp.zeros((rows, outs), F32) if p is None else p for p in line], axis=1
                )
            )
        return jnp.concatenate(bands, axis=0).astype(BF)

    for k in range(2):
        pieces = [
            [w2[k, ci % 2].astype(F32) if ci // 2 == co else None for co in range(4)]
            for ci in range(8)
        ]
        e2[256 * k : 256 * k + 256] = spread(pieces, 32, 64, 4)
        pieces = [
            [w3[k, ci % 2].astype(F32) if ci // 2 == co else None for co in range(2)]
            for ci in range(4)
        ]
        e3[256 * k : 256 * k + 256] = spread(pieces, 64, 64, 2)
    e4[...] = spread(
        [[w4[...].astype(F32) if ci == co else None for co in range(4)] for ci in range(4)], 64, 64, 4
    )
    e5[...] = spread(
        [[jnp.transpose(w5[...].astype(F32)) if ci == co else None for co in range(4)] for ci in range(4)], 64, 32, 4
    )


def relu(x):
    return jnp.maximum(x, 0.0).astype(BF)


def encode_chunk(px, xs, a1, a2, a3, e1, e2, e3, e4, e5, perm):
    for part in range(CHUNK // 32):
        sorted_rows = dot(perm[...], px[part * 256 : part * 256 + 256, :]).astype(BF)
        for k in range(8):
            xs[k // 2, part * 32 : part * 32 + 32, (k % 2) * 128 : (k % 2) * 128 + 128] = sorted_rows[
                k * 32 : k * 32 + 32
            ]
    lhs = xs[...].reshape(4 * CHUNK, 256)
    for j in range(4):
        out = relu(dot(lhs, e1[:, 512 * j : 512 * j + 512]))
        out = out.reshape(2, 2, CHUNK, 512)
        for half in range(2):
            for k2 in range(2):
                a1[2 * j + half, :, 256 * k2 : 256 * k2 + 256] = out[
                    :, k2, :, 256 * half : 256 * half + 256
                ].reshape(2 * CHUNK, 256)
    for j in range(2):
        out = relu(dot(a1[4 * j : 4 * j + 4].reshape(8 * CHUNK, 512), e2[...]))
        out = out.reshape(4, 2, CHUNK, 256)
        for k3 in range(2):
            a2[4 * j : 4 * j + 4, :, 256 * k3 : 256 * k3 + 256] = out[:, k3]
    out = relu(dot(a2[...].reshape(8 * CHUNK, 512), e3[...])).reshape(4, 2, CHUNK, 128)
    a3[:, :, 0:128] = out[:, 0]
    a3[:, :, 128:256] = out[:, 1]
    out = relu(dot(a3[...].reshape(4 * CHUNK, 256), e4[...]))
    out = dot(out, e5[...]).astype(BF).reshape(4, CHUNK // 16, 16, 128)
    return jnp.stack([out[:, k] for k in range(CHUNK // 16)])


def share_kernel(
    px_hbm, w1_hbm, w2_hbm, w3_hbm, w4_hbm, w5_hbm, cur, prior,
    px, w1, w2, w3, w4, w5, bands, xs, a1, a2, a3, e1, e2, e3, e4, e5, perm,
    load_sem, px_sem, send_sem, cur_sem, prior_sem, halo_send, halo_recv, home_sem,
):
    s = lax.axis_index("sec")
    t = lax.axis_index("tile")
    secs = lax.axis_size("sec")
    tiles = lax.axis_size("tile")
    group = lax.rem(t, 4)
    member = lax.div(t, 4)
    chunks = ROWS // CHUNK
    pixels = 8 * CHUNK

    def chunk_at(phase):
        flip = jnp.int32(chunks - 1) - phase
        high = lax.rem(lax.div(member, 2) + lax.div(flip, 2), 2)
        return 2 * high + lax.rem(member + flip, 2)


    barrier = pltpu.get_barrier_semaphore()

    def greet(to_s, to_t):
        pl.semaphore_signal(
            barrier, inc=1, device_id=(to_s, to_t), device_id_type=pl.DeviceIdType.MESH
        )

    @pl.loop(1, tiles, unroll=True)
    def _(k):
        greet(s, lax.rem(t + k, tiles))

    @pl.when(s > 0)
    def _():
        @pl.loop(0, tiles, unroll=True)
        def _(k):
            greet(s - 1, lax.rem(t + k, tiles))

    loads = [
        pltpu.make_async_copy(a, b, load_sem.at[i])
        for i, (a, b) in enumerate(
            [(w1_hbm, w1), (w2_hbm, w2), (w3_hbm, w3), (w4_hbm, w4), (w5_hbm, w5)]
        )
    ]
    for load in loads:
        load.start()

    def fetch(phase):
        chunk = chunk_at(phase)
        return pltpu.make_async_copy(
            px_hbm.at[0, pl.ds(pl.multiple_of(chunk * pixels, pixels), pixels)],
            px.at[phase],
            px_sem.at[phase],
        )

    for phase in range(chunks):
        fetch(phase).start()

    r = iota((256, 256), 0)
    c = iota((256, 256), 1)
    perm[...] = jnp.where(8 * (r % 32) + r // 32 == c, 1.0, 0.0).astype(BF)
    for load in loads:
        load.wait()
    expand_weights(w1, w2, w3, w4, w5, e1, e2, e3, e4, e5)

    def band_of(to_t):
        return bands.at[to_t]

    home = pltpu.make_async_copy(band_of(t), cur.at[member, group], home_sem)

    def encode_phase(phase):
        chunk = chunk_at(phase)
        fetch(phase).wait()
        done = encode_chunk(px.at[phase], xs, a1, a2, a3, e1, e2, e3, e4, e5, perm)
        bands[pl.ds(chunk * (CHUNK // 16), CHUNK // 16)] = done

    def send_phase(phase):
        chunk = chunk_at(phase)

        def push(to_t, to_s, by, dst, sem):
            pltpu.make_async_remote_copy(
                src_ref=band_of(to_t),
                dst_ref=dst,
                send_sem=send_sem.at[by],
                recv_sem=sem,
                device_id=to_s,
                device_id_type=pl.DeviceIdType.MESH,
            ).start()

        @pl.when(s < secs - 1)
        def _():
            @pl.loop(0, CHUNK // 16)
            def _(k):
                to_t = chunk * (CHUNK // 16) + lax.rem(k + member, CHUNK // 16)
                push(to_t, (s + 1, to_t), 0, prior.at[1, member, group], prior_sem.at[member])

                @pl.when(to_t == tiles // 2 - 1)
                def _():
                    push(to_t, (s + 1, to_t + 1), 2, prior.at[0, member, group], halo_recv.at[0, member])

                @pl.when(to_t == tiles // 2)
                def _():
                    push(to_t, (s + 1, to_t - 1), 2, prior.at[2, member, group], halo_recv.at[1, member])

        @pl.loop(0, CHUNK // 16)
        def _(k):
            to_t = chunk * (CHUNK // 16) + lax.rem(k + member, CHUNK // 16)

            @pl.when(to_t != t)
            def _():
                push(to_t, (s, to_t), 1, cur.at[member, group], cur_sem.at[0])

            @pl.when(to_t == t)
            def _():
                home.start()

    @pl.loop(0, chunks)
    def _(phase):
        encode_phase(phase)

        @pl.when(phase == HELD - 1)
        def _():
            @pl.when(s < secs - 1)
            def _():
                pl.semaphore_wait(barrier, 2 * tiles - 1)

            @pl.when(s == secs - 1)
            def _():
                pl.semaphore_wait(barrier, tiles - 1)

            @pl.loop(0, HELD)
            def _(before):
                send_phase(before)

        @pl.when(phase >= HELD)
        def _():
            send_phase(phase)

    def halo(to_t, part, side, g):
        return pltpu.make_async_remote_copy(
            src_ref=prior.at[1, g],
            dst_ref=prior.at[part, g],
            send_sem=halo_send.at[side, g],
            recv_sem=halo_recv.at[side, g],
            device_id=(s, to_t),
            device_id_type=pl.DeviceIdType.MESH,
        )

    has_next = t < tiles - 1
    has_last = t > 0

    def arrive(ref, sem):
        pltpu.make_async_copy(ref, ref, sem).wait()

    @pl.when(s > 0)
    def _():
        @pl.loop(0, 4)
        def _(k):
            g = chunk_at(k)
            arrive(prior.at[1, g], prior_sem.at[g])

            @pl.when(has_next & (t != tiles // 2 - 1))
            def _():
                halo(t + 1, 0, 0, g).start()

            @pl.when(has_last & (t != tiles // 2))
            def _():
                halo(t - 1, 2, 1, g).start()

    home.wait()
    arrive(bands.at[0:15], cur_sem.at[0])
    arrive(bands.at[0:15], send_sem.at[1])

    @pl.when(s < secs - 1)
    def _():
        arrive(bands, send_sem.at[0])
        arrive(bands.at[0:2], send_sem.at[2])

    @pl.when(s > 0)
    def _():
        @pl.loop(0, 4)
        def _(g):
            @pl.when(has_next & (t != tiles // 2 - 1))
            def _():
                halo(t + 1, 0, 0, g).wait_send()

            @pl.when(has_last & (t != tiles // 2))
            def _():
                halo(t - 1, 2, 1, g).wait_send()

            @pl.when(has_next)
            def _():
                arrive(prior.at[2, g], halo_recv.at[1, g])

            @pl.when(has_last)
            def _():
                arrive(prior.at[0, g], halo_recv.at[0, g])


def share(sections, weights):
    hbm = pl.BlockSpec(memory_space=pltpu.HBM)
    return pl.pallas_call(
        share_kernel,
        out_shape=(
            jax.ShapeDtypeStruct((4, 4, 4, 16, 128), BF),
            jax.ShapeDtypeStruct((3, 4, 4, 4, 16, 128), BF),
        ),
        in_specs=[hbm] * 6,
        out_specs=(hbm, hbm),
        scratch_shapes=[
            pltpu.VMEM((ROWS // CHUNK, 8 * CHUNK, 128), BF),
            *[pltpu.VMEM(w.shape, BF) for w in weights],
            pltpu.VMEM((ROWS // 16, 4, 16, 128), BF),
            pltpu.VMEM((4, CHUNK, 256), BF),
            pltpu.VMEM((8, 2 * CHUNK, 512), BF),
            pltpu.VMEM((8, CHUNK, 512), BF),
            pltpu.VMEM((4, CHUNK, 256), BF),
            pltpu.VMEM((256, 2048), BF),
            pltpu.VMEM((512, 256), BF),
            pltpu.VMEM((512, 128), BF),
            pltpu.VMEM((256, 256), BF),
            pltpu.VMEM((256, 128), BF),
            pltpu.VMEM((256, 256), BF),
            pltpu.SemaphoreType.DMA((5,)),
            pltpu.SemaphoreType.DMA((ROWS // CHUNK,)),
            pltpu.SemaphoreType.DMA((3,)),
            pltpu.SemaphoreType.DMA((1,)),
            pltpu.SemaphoreType.DMA((4,)),
            pltpu.SemaphoreType.DMA((2, 4)),
            pltpu.SemaphoreType.DMA((2, 4)),
            pltpu.SemaphoreType.DMA,
        ],
        compiler_params=pltpu.CompilerParams(
            vmem_limit_bytes=LIMIT, collective_id=0, has_side_effects=True
        ),
        name="share",
    )(sections, *weights)


def weave(main, *others):
    extra = [step for other in others for step in other]
    used = 0
    for n, step in enumerate(main):
        step()
        goal = len(extra) * (n + 1) // len(main)
        while used < goal:
            extra[used]()
            used += 1


def correlate_kernel(
    shift, cur_hbm, prior_hbm, out_hbm, cur, prior, cur32, wide, both, above, below, rhs, picked, rows, out, in_sem, out_sem
):
    s = lax.axis_index("sec")
    t = lax.axis_index("tile")
    loads = []
    for i in range(4):
        near = pl.ds(16 * i, 16)
        loads.append(
            (
                pltpu.make_async_copy(prior_hbm.at[:, near], prior.at[:, near], in_sem.at[0, i]),
                pltpu.make_async_copy(cur_hbm.at[near], cur.at[near], in_sem.at[1, i]),
            )
        )
    for pair in loads:
        for load in pair:
            load.start()
    wide[0:4] = jnp.zeros((4, 48, 128), F32)
    wide[68:72] = jnp.zeros((4, 48, 128), F32)

    inside = [(s > 0) & (t > 0), s > 0, (s > 0) & (t < lax.axis_size("tile") - 1)]

    lane = iota((8, 128), 1)
    slot = lane // 32
    sub = iota((8, 128), 0)
    lane256 = iota((8, 256), 1)
    block = (lane256 % 32) // 8
    wide_lane = iota((32, 128), 1)

    def widen(member):
        def step(i):
            if i == 0:
                for load in loads[member]:
                    load.wait()
            q = 16 * member + 4 * i
            for part in range(3):
                values = prior[part, q : q + 4].astype(F32)
                wide[4 + q : 8 + q, 16 * part : 16 * part + 16] = jnp.where(inside[part], values, 0.0)
            cur32[q : q + 4] = cur[q : q + 4].astype(F32)

        return [functools.partial(step, i) for i in range(4)]

    def windows(tile):
        dy = shift[0, tile]
        kept = {}

        def step(q):
            here = wide[16 * tile + q, pl.ds(8 + dy, 32), :]
            beside = wide[16 * tile + q + 1, pl.ds(8 + dy, 32), :]
            kept[q] = [here]
            for e in range(1, 4):
                mixed = jnp.where(wide_lane < 32 * e, beside, here)
                kept[q].append(pltpu.roll(mixed, 128 - 32 * e, 1))
            for e in range(4):
                both[tile][e, q] = kept[q][e][8:24].astype(BF)
            for first in [q - 2] + ([q - 1, q] if q == 22 else []):
                if first >= 0:
                    second = min(first + 2, 22)
                    for e in range(4):
                        for rows_of, at in ((above, 0), (below, 24)):
                            pair = [kept[first][e][at : at + 8], kept[second][e][at : at + 8]]
                            rows_of[tile][e, first] = jnp.concatenate(pair, axis=0).astype(BF)

        return [functools.partial(step, q) for q in range(23)]

    def masked(side, j):
        def step(u):
            y = (u % 4 - j) % 4 + 4 * (u // 4)
            for pair in range(2):
                left, right = [], []
                for m in (2 * pair, 2 * pair + 1):
                    q = 32 * side + 8 * j + 2 * m
                    a = jnp.broadcast_to(cur32[q, y : y + 1, :], (8, 128))
                    b = jnp.broadcast_to(cur32[q + 1, y : y + 1, :], (8, 128))
                    left.append(jnp.where(slot == sub, a, 0.0))
                    right.append(jnp.where(slot + 4 == sub, b, 0.0))
                at = u * 32 + 16 * pair
                rhs[j % 2][at : at + 16, 0:128] = jnp.concatenate(left, axis=0).astype(BF)
                rhs[j % 2][at : at + 16, 128:256] = jnp.concatenate(right, axis=0).astype(BF)

        return [functools.partial(step, u) for u in range(16)]

    def products(side, j):
        tile = 2 * side + j // 2
        dx = shift[1, tile]

        def times(parts, weights):
            return lax.dot_general(
                jnp.concatenate(parts, axis=0),
                weights,
                (((1,), (1,)), ((), ())),
                preferred_element_type=F32,
            ).reshape(len(parts), 2, 8, weights.shape[0])

        def step(group):
            places, parts, pairs, tops, ends = [], [], [], [], []
            for jj in group:
                place = 8 + dx + 32 * (j % 2) + jj
                e = lax.rem(place, 4)
                q = lax.div(place, 4)

                def window(source, m):
                    return jnp.concatenate([source[tile][e, q + 2 * m], source[tile][e, q + 2 * m + 1]], axis=1)

                for m in range(6 if jj == 0 else 5):
                    places.append(jj + 8 * m)
                    parts.append(window(both, m))
                for m in range(0, 6, 2):
                    pairs += [jj + 8 * m, jj + 8 * m + 8]
                    tops.append(window(above, m))
                    ends.append(window(below, m))
            weights = rhs[j % 2]
            middle = times(parts, weights[...])
            top = times(tops, weights[0:256])
            end = times(ends, weights[256:512])

            def rows_at(place, half, i):
                if i + half == 0:
                    return top[pairs.index(place) // 2, pairs.index(place) % 2]
                if i + half == 3:
                    return end[pairs.index(place) // 2, pairs.index(place) % 2]
                return middle[places.index(place), i + half - 1, :, 256 * half : 256 * half + 256]

            for jj in group:
                for ox in range(jj, SPAN, 8):
                    for half in range(2):
                        for i in range(3):
                            piece = rows_at(ox + 24, half, i)
                            for b in (2, 1, 0):
                                piece = jnp.where(block == b, rows_at(ox + 8 * b, half, i), piece)
                            picked[2 * side + half][j, ox, i] = piece

        return [functools.partial(step, range(g, g + GROUP)) for g in range(0, 8, GROUP)]

    def merge(side, half):
        source = picked[2 * side + half]

        def step(ox):
            for v in range(2):
                for i in range(3):
                    blocks = [source[j, ox, i, :, 128 * v : 128 * v + 128] for j in range(4)]
                    for k in range(4):
                        merged = blocks[(3 - k) % 4]
                        for u in (2, 1, 0):
                            merged = jnp.where(slot == u, blocks[(u - k) % 4], merged)
                        if k:
                            merged = pltpu.roll(merged, 128 - 32 * k, 1)
                        y = 4 * v + k
                        start = (BASE + 8 * i - y) * LINE + ox * 8 + y
                        rows[half][pl.ds(start, 8, stride=LINE), :] = merged

        return [functools.partial(step, ox) for ox in range(SPAN)]

    sends = []

    def finish(side, half):
        def step(oy):
            start = (BASE + oy) * LINE
            done = rows[half][start : start + SPAN * 8, :] * (1.0 / math.sqrt(32))
            done = done.astype(BF).reshape(SPAN, 8, 128)
            out[side, oy * SPAN : oy * SPAN + SPAN, 8 * half : 8 * half + 8, :] = done
            if half == 1 and (oy + 1) in SENT:
                part = SENT.index(oy + 1)
                begin = SENT[part - 1] * SPAN if part else 0
                span = pl.ds(begin, (oy + 1) * SPAN - begin)
                send = pltpu.make_async_copy(
                    out.at[side, span],
                    out_hbm.at[span, :, pl.ds(128 * side, 128)],
                    out_sem.at[side, part],
                )
                send.start()
                sends.append(send)

        return [functools.partial(step, oy) for oy in range(SPAN)]

    def run(steps):
        for step in steps:
            step()

    def stage(side, extra, following):
        for j in range(4):
            after = masked(side, j + 1) if j < 3 else following
            weave(products(side, j), after, extra[j])

    def quarters(steps):
        return [steps[len(steps) * n // 4 : len(steps) * (n + 1) // 4] for n in range(4)]

    run(widen(0))
    run(widen(1))
    run(masked(0, 0))
    run(windows(0))
    beside = windows(1)
    stage(
        0, [widen(2) + beside[:11], beside[11:] + widen(3), windows(2), windows(3)], masked(1, 0),
    )
    stage(1, quarters(merge(0, 0) + finish(0, 0) + merge(0, 1) + finish(0, 1)), [])
    for half in range(2):
        run(merge(1, half))
        run(finish(1, half))
    for send in sends:
        send.wait()


def correlate(current, prior, tile_shift):
    hbm = pl.BlockSpec(memory_space=pltpu.HBM)
    return pl.pallas_call(
        correlate_kernel,
        out_shape=jax.ShapeDtypeStruct((OFFSETS, 16, 256), BF),
        in_specs=[pl.BlockSpec(memory_space=pltpu.SMEM), hbm, hbm],
        out_specs=hbm,
        scratch_shapes=[
            pltpu.VMEM((64, 16, 128), BF),
            pltpu.VMEM((3, 64, 16, 128), BF),
            pltpu.VMEM((64, 16, 128), F32),
            pltpu.VMEM((72, 48, 128), F32),
            [pltpu.VMEM((4, 24, 16, 128), BF)] * 4,
            [pltpu.VMEM((4, 24, 16, 128), BF)] * 4,
            [pltpu.VMEM((4, 24, 16, 128), BF)] * 4,
            [pltpu.VMEM((512, 256), BF)] * 2,
            [pltpu.VMEM((4, SPAN, 3, 8, 256), F32)] * 4,
            [pltpu.VMEM(((BASE + 25) * LINE, 128), F32)] * 2,
            pltpu.VMEM((2, OFFSETS, 16, 128), BF),
            pltpu.SemaphoreType.DMA((2, 4)),
            pltpu.SemaphoreType.DMA((2, len(SENT))),
        ],
        compiler_params=pltpu.CompilerParams(vmem_limit_bytes=LIMIT),
        name="correlate",
    )(tile_shift, current, prior)


def local(sections, tile_shift, w_first, w_second, w_third, w_fourth, w_fifth):
    weights = (w_first.reshape(2, 2, 32), w_second, w_third, w_fourth, w_fifth.T)
    current, prior = share(sections, weights)
    current = current.reshape(64, 16, 128)
    prior = prior.reshape(3, 64, 16, 128)
    shift = jnp.transpose(tile_shift, (0, 1, 3, 2)).reshape(2, 4)
    found = correlate(current, prior, shift)
    return jnp.transpose(found[None], (0, 2, 1, 3))


def solution(mesh):
    placed = (P("sec", None, "tile"), P("sec", "tile", None, None), P(), P(), P(), P(), P())
    return jax.shard_map(
        local, mesh=mesh, in_specs=placed, out_specs=P("sec", "tile", None, None), check_vma=False
    )
```
